32 devices in a mesh: segment: 4 (over x, core), seq: 2 (over y), mp: 4 (over z).
Axes of the slice: x: 2, y: 2, z: 4, core: 2. Of those that a mesh axis runs over, the one named last changes fastest.
Arguments:
- captions: bfloat16 [16, 128, 4096], P('seq', None, 'segment'), may hold values from -6 to 6
- caption_lengths: int32 [16], replicated, may hold values from 1 to 128, as said below
- image_caption: int32 [16], replicated, may hold values from 0 to 15, each once
- t5_gain: float32 [4096], P('segment'), may hold values from 0.25 to 1.75
- w_key: bfloat16 [4096, 4096], P('segment', 'mp'), may hold values from -0.09375 to 0.09375
- w_value: bfloat16 [4096, 4096], P('segment', 'mp'), may hold values from -0.09375 to 0.09375
- queries: bfloat16 [16, 512, 4096], P('segment', 'seq', 'mp'), may hold values from -300 to 300
- hidden: bfloat16 [16, 512, 4096], P('segment', 'seq', 'mp'), may hold values from -1.5 to 1.5
- out_gate: float32 [16, 4096], P('segment', 'mp'), may hold values from 1 to 4
- w_out: bfloat16 [4096, 4096], P('mp', 'seq'), may hold values from -0.09375 to 0.09375
Outputs:
- result_rows: bfloat16 [16, 512, 4096], P('segment', 'seq', 'mp')
The draws below stay inside these ranges and needn't reach their ends.
Inputs may be any that keep to these rules, and one draw needn't show every extreme that they name: `caption_lengths`: each caption has at least one live token, and some caption fills all 128 slots.
All inputs are finite; a program needn't handle non-finite values.
Results may differ from the reference program's by a relative error of at most 0.03.
Values may be sent and summed in bfloat16 or wider, within the bound.
A program may use at most 128 MiB of HBM per device.

```python
import jax
import jax.numpy as jnp
from jax import lax

D = 4096
HEADS = 32
HEAD = 128
CAP_LEN = 128
LENGTH = 512
IMAGES = 16
CAPTIONS = 16
N_MP = 4


def draw_caption_lengths(key, part):
    drawn = jax.random.randint(key, (CAPTIONS,), 1, CAP_LEN + 1)
    longest = jax.random.randint(jax.random.fold_in(key, 7), (), 0, CAPTIONS)
    filled = jnp.where(jnp.arange(CAPTIONS, dtype=jnp.int32) == longest, CAP_LEN, drawn)
    return filled.astype(jnp.int32)


def draw_queries(key, part):
    base = jax.random.normal(key, (IMAGES, LENGTH, D), jnp.float32) * 1.5
    return jnp.clip(base, -300.0, 300.0).astype(jnp.bfloat16)


def steps_of(rng, dims, cuts, low, top_value):
    level = 1.0
    for position, parts in cuts:
        steps = jax.random.uniform(jax.random.fold_in(jax.random.fold_in(rng, 6), position), (parts,), jnp.float32, low / len(cuts), top_value / len(cuts))
        level = level * jnp.repeat(jnp.exp(steps), dims[position] // parts).reshape((-1,) + (1,) * (len(dims) - 1 - position))
    return level


def noise(stream_key, dims, scale, reach, cuts=(), held_as=jnp.bfloat16):
    loudness = steps_of(stream_key, dims, cuts, -0.22, 0.18) if cuts else 1.0
    array = jax.random.normal(stream_key, dims, jnp.float32) * scale * loudness
    return jnp.minimum(jnp.maximum(array, -reach), reach).astype(held_as)


def setup_inputs(seed: int = 0) -> dict:
    seeds = jax.random.split(jax.random.key(seed), 11)
    captions = noise(seeds[0], (CAPTIONS, CAP_LEN, D), 1.0, 6.0, ((0, 2), (2, 4)))
    caption_lengths = draw_caption_lengths(jax.random.fold_in(seeds[10], 71), 0)
    image_caption = jax.random.permutation(seeds[2], IMAGES).astype(jnp.int32)
    t5_gain = jnp.clip(1.0 + 0.15 * jax.random.normal(seeds[3], (D,), jnp.float32), 0.25, 1.75)
    w_key = noise(seeds[4], (D, D), D ** -0.5, 0.09375, ((0, 4), (1, 4)))
    w_value = noise(seeds[5], (D, D), D ** -0.5, 0.09375, ((0, 4), (1, 4)))
    queries = draw_queries(jax.random.fold_in(seeds[10], 71), 0)
    hidden = noise(seeds[7], (IMAGES, LENGTH, D), 0.25, 1.5, ((0, 4), (1, 2), (2, 4)))
    out_gate = jnp.clip(1.0 + 3.0 * jax.random.uniform(seeds[8], (IMAGES, D), jnp.float32) ** steps_of(seeds[8], (IMAGES, D), ((0, 4), (1, 4)), -0.2, 0.2), 1.0, 4.0)
    w_out = noise(seeds[9], (D, D), D ** -0.5, 0.09375, ((0, 4), (1, 2)))
    return {"captions": captions, "caption_lengths": caption_lengths, "image_caption": image_caption, "t5_gain": t5_gain, "w_key": w_key, "w_value": w_value, "queries": queries, "hidden": hidden, "out_gate": out_gate, "w_out": w_out}


def reference(captions, caption_lengths, image_caption, t5_gain, w_key, w_value, queries, hidden, out_gate, w_out):
    caption_values = captions.astype(jnp.float32)
    mean_square = lax.optimization_barrier(jnp.mean(caption_values * caption_values, axis=2, keepdims=True))
    normed = (caption_values * lax.rsqrt(mean_square + 1e-06) * t5_gain).astype(jnp.bfloat16)
    flattened = normed.reshape(CAPTIONS * CAP_LEN, D)
    key_rows = jnp.dot(flattened, w_key, preferred_element_type=jnp.float32).astype(jnp.bfloat16).reshape(CAPTIONS, CAP_LEN, D)
    value_rows = jnp.dot(flattened, w_value, preferred_element_type=jnp.float32).astype(jnp.bfloat16).reshape(CAPTIONS, CAP_LEN, D)
    group_width = D // N_MP

    def per_image(image):
        caption = image_caption[image]
        key_heads = jnp.take(key_rows, caption, axis=0).reshape(CAP_LEN, HEADS, HEAD).astype(jnp.float32)
        value_heads = jnp.take(value_rows, caption, axis=0).reshape(CAP_LEN, HEADS, HEAD).astype(jnp.float32)
        query_heads = jnp.take(queries, image, axis=0).reshape(LENGTH, HEADS, HEAD).astype(jnp.float32)
        scores = jnp.einsum('phd,khd->hpk', query_heads, key_heads) * HEAD ** (-0.5)
        live_mask = jnp.arange(CAP_LEN, dtype=jnp.int32) < jnp.take(caption_lengths, caption)
        scores = jnp.where(live_mask[None, None, :], scores, -1e+30)
        weights = jax.nn.softmax(scores, axis=2).astype(jnp.bfloat16)
        attended = jnp.einsum('hpk,khd->phd', weights.astype(jnp.float32), value_heads)
        attended = attended.astype(jnp.bfloat16).reshape(LENGTH, D)
        projected = jnp.zeros((LENGTH, D), jnp.float32)
        for group in range(N_MP):
            partial_value = jnp.dot(attended[:, group * group_width:(group + 1) * group_width], w_out[group * group_width:(group + 1) * group_width], preferred_element_type=jnp.float32)
            projected = projected + lax.optimization_barrier(partial_value.astype(jnp.bfloat16)).astype(jnp.float32)
        gate_row = jnp.take(out_gate, image, axis=0)
        residual = jnp.take(hidden, image, axis=0).astype(jnp.float32)
        return (residual + gate_row[None, :] * projected).astype(jnp.bfloat16)
    return lax.map(per_image, jnp.arange(IMAGES, dtype=jnp.int32))
```

```python
import functools

import jax
import jax.numpy as jnp
from jax import lax
from jax.experimental import pallas as pl
from jax.experimental.pallas import tpu as pltpu
from jax.sharding import PartitionSpec as P

HEAD = 128
MESH = pl.DeviceIdType.MESH
BF16 = jnp.bfloat16
F32 = jnp.float32


def general_shards(
    captions,
    caption_lengths,
    image_caption,
    t5_gain,
    w_key,
    w_value,
    queries,
    hidden,
    out_gate,
    w_out,
):
    caption_count, caption_slots, feature_share = captions.shape
    image_count, patch_count, head_cols = queries.shape
    segment_count = lax.axis_size("segment")
    caption_values = captions.astype(jnp.float32)
    squares_total = lax.psum(jnp.sum(caption_values * caption_values, axis=2), "segment")
    inverse_rms = lax.rsqrt(squares_total / (feature_share * segment_count) + 1e-06)
    normed = (caption_values * inverse_rms[:, :, None] * t5_gain).astype(jnp.bfloat16)
    flattened = normed.reshape(caption_count * caption_slots, feature_share)
    key_partial = jnp.dot(flattened, w_key, preferred_element_type=jnp.float32)
    value_partial = jnp.dot(flattened, w_value, preferred_element_type=jnp.float32)
    first_image = lax.axis_index("segment") * image_count
    owner_ids = lax.dynamic_slice_in_dim(image_caption, first_image, image_count)
    stacked = jnp.concatenate([key_partial, value_partial], axis=1)
    column_share = lax.psum_scatter(
        stacked.astype(jnp.bfloat16), "segment", scatter_dimension=1, tiled=True
    ).astype(jnp.float32)
    piece_width = column_share.shape[1]
    column_share = column_share.astype(jnp.bfloat16).reshape(
        1, caption_count, caption_slots, piece_width
    )
    pieces = lax.all_gather(column_share, ("segment", "seq"), axis=0, tiled=True)
    pieces = pieces.reshape(segment_count, -1, caption_slots, piece_width)
    encoded = pieces.transpose(1, 2, 0, 3).reshape(
        pieces.shape[1], caption_slots, segment_count * piece_width
    )
    chosen = jnp.take(encoded, owner_ids, axis=0)
    live_lengths = jnp.take(caption_lengths, owner_ids)
    live_mask = jnp.arange(caption_slots, dtype=jnp.int32)[None, :] < live_lengths[:, None]
    head_count = head_cols // HEAD
    query_heads = queries.reshape(image_count, patch_count, head_count, HEAD)
    key_heads = chosen[:, :, :head_cols].reshape(image_count, caption_slots, head_count, HEAD)
    value_heads = chosen[:, :, head_cols:].reshape(image_count, caption_slots, head_count, HEAD)
    scores = jnp.einsum(
        "iphd,ikhd->ihpk", query_heads, key_heads, preferred_element_type=jnp.float32
    ) * HEAD ** (-0.5)
    scores = jnp.where(live_mask[:, None, None, :], scores, -1e30)
    weights = jax.nn.softmax(scores, axis=3).astype(jnp.bfloat16)
    attended = jnp.einsum(
        "ihpk,ikhd->iphd", weights, value_heads, preferred_element_type=jnp.float32
    )
    attended = attended.astype(jnp.bfloat16).reshape(image_count * patch_count, head_cols)
    partial_value = jnp.dot(
        attended,
        lax.all_gather(w_out, "seq", axis=1, tiled=True),
        preferred_element_type=jnp.float32,
    )
    mixed_heads = lax.psum_scatter(
        partial_value.astype(jnp.bfloat16), "mp", scatter_dimension=1, tiled=True
    ).astype(jnp.float32)
    result_rows = hidden.astype(jnp.float32) + out_gate[:, None, :] * mixed_heads.reshape(
        image_count, patch_count, head_cols
    )
    return result_rows.astype(jnp.bfloat16)


def fused_kernel(
    image_caption, caption_lengths, gain, gate, captions, w_key, w_value, queries, hidden, w_out,
    result,
    cap_raw, key_w, value_w, query_v, hidden_v, out_w, scaled, squares,
    pair_send, pair_recv, own, cross_recv, rows, attended, moving, from_right,
    local_sem, pair_ssem, pair_rsem, cross_ssem, cross_rsem, row_ssem, row_rsem,
    w_ssem, w_rsem, wf_ssem, wf_rsem, z_ssem, z_rsem, left_rsem,
):
    seg = lax.axis_index("segment")
    seq = lax.axis_index("seq")
    mp = lax.axis_index("mp")
    chip, core = seg // 2, seg % 2
    pair_id = {"segment": seg + 1 - 2 * core}
    cross_id = {"segment": (seg + 2) % 4}
    seq_id = {"seq": 1 - seq}
    caption_count, slots, features = cap_raw.shape
    images, patches, width = query_v.shape
    both = 2 * width
    head_count = width // HEAD
    half = out_w.shape[1] // 2
    total_features = 4 * features

    def device(ids):
        return {"segment": seg, "seq": seq, "mp": mp, **ids}

    loads = [
        pltpu.make_async_copy(captions, cap_raw, local_sem.at[0]),
        pltpu.make_async_copy(w_key, key_w, local_sem.at[1]),
        pltpu.make_async_copy(w_value, value_w, local_sem.at[2]),
        pltpu.make_async_copy(queries, query_v, local_sem.at[3]),
        pltpu.make_async_copy(
            w_out.at[:, pl.ds(0, width)], out_w.at[2 * seq], local_sem.at[4]
        ),
        pltpu.make_async_copy(
            w_out.at[:, pl.ds(width, width)], out_w.at[2 * seq + 1], local_sem.at[5]
        ),
        pltpu.make_async_copy(hidden, hidden_v, local_sem.at[6]),
    ]
    for load in loads:
        load.start()

    barrier = pltpu.get_barrier_semaphore()
    for ids in (pair_id, cross_id, seq_id):
        pl.semaphore_signal(barrier, inc=1, device_id=device(ids), device_id_type=MESH)

    @pl.when(mp > 0)
    def _():
        pl.semaphore_signal(barrier, inc=1, device_id=device({"mp": mp - 1}), device_id_type=MESH)

    @pl.when(mp < 3)
    def _():
        pl.semaphore_signal(barrier, inc=1, device_id=device({"mp": mp + 1}), device_id_type=MESH)

    neighbours = 5 - (mp == 0).astype(jnp.int32) - (mp == 3).astype(jnp.int32)
    pl.semaphore_wait(barrier, neighbours)

    half_rows = pl.ds(pl.multiple_of(core * half, half), half)

    def w_copy(step):
        local_block = seq if step == 0 else 1 - seq
        block = 2 * seq + local_block
        return pltpu.make_async_remote_copy(
            src_ref=w_out.at[half_rows, pl.ds(pl.multiple_of(local_block * width, width), width)],
            dst_ref=out_w.at[block, half_rows],
            send_sem=w_ssem.at[step],
            recv_sem=w_rsem.at[step],
            device_id=device(seq_id),
            device_id_type=MESH,
        )

    def w_forward(step):
        other = 1 - seq
        block = 2 * other + (other if step == 0 else 1 - other)
        return pltpu.make_async_remote_copy(
            src_ref=out_w.at[block, half_rows],
            dst_ref=out_w.at[block, half_rows],
            send_sem=wf_ssem.at[step],
            recv_sem=wf_rsem.at[step],
            device_id=device(pair_id),
            device_id_type=MESH,
        )

    w_copy(0).start()

    loads[0].wait()

    @pl.loop(0, caption_count)
    def _(c):
        values = cap_raw[c].astype(F32)
        scaled[c] = (values * gain[...]).astype(BF16)
        square = values * values
        folded = square[:, :HEAD]
        for group in range(1, features // HEAD):
            folded = folded + square[:, group * HEAD : (group + 1) * HEAD]
        squares[c] = folded.astype(BF16)

    loads[1].wait()
    loads[2].wait()
    tile = 256

    def slot_partial(j, out_core, dst):
        ids = [image_caption[4 * (2 * x + out_core) + j] % caption_count for x in range(2)]
        lhs = jnp.concatenate([scaled[i] for i in ids], axis=0)

        @pl.loop(0, width // tile)
        def _(t):
            cols = pl.ds(pl.multiple_of(t * tile, tile), tile)
            vcols = pl.ds(pl.multiple_of(width + t * tile, tile), tile)
            k = jnp.dot(lhs, key_w[:, cols], preferred_element_type=F32).astype(BF16)
            v = jnp.dot(lhs, value_w[:, cols], preferred_element_type=F32).astype(BF16)
            for x in range(2):
                dst[j, x, :, cols] = k[x * slots : (x + 1) * slots]
                dst[j, x, :, vcols] = v[x * slots : (x + 1) * slots]

        for x in range(2):
            dst[j, x, :, both:] = squares[ids[x]]

    def pair_copy(j):
        return pltpu.make_async_remote_copy(
            src_ref=pair_send.at[j], dst_ref=pair_recv.at[j],
            send_sem=pair_ssem.at[j], recv_sem=pair_rsem.at[j],
            device_id=device(pair_id), device_id_type=MESH,
        )

    def cross_copy(j):
        return pltpu.make_async_remote_copy(
            src_ref=own.at[j, 1 - chip], dst_ref=cross_recv.at[j],
            send_sem=cross_ssem.at[j], recv_sem=cross_rsem.at[j],
            device_id=device(cross_id), device_id_type=MESH,
        )

    def row_copy(j):
        return pltpu.make_async_remote_copy(
            src_ref=rows.at[j, seq], dst_ref=rows.at[j, seq],
            send_sem=row_ssem.at[j], recv_sem=row_rsem.at[j],
            device_id=device(seq_id), device_id_type=MESH,
        )

    def stage_partial(j):
        slot_partial(j, 1 - core, pair_send)
        pair_copy(j).start()
        slot_partial(j, core, own)

    def stage_pair(j):
        pair_copy(j).wait_recv()
        far = 1 - chip
        own[j, far] = (own[j, far].astype(F32) + pair_recv[j, far].astype(F32)).astype(BF16)
        cross_copy(j).start()

    def stage_rows(j):
        cross_copy(j).wait_recv()
        sums = [ref[...].astype(F32) for ref in (
            own.at[j, chip, :, pl.ds(both, HEAD)],
            pair_recv.at[j, chip, :, pl.ds(both, HEAD)],
            cross_recv.at[j, :, pl.ds(both, HEAD)],
        )]
        mean = jnp.sum(sums[0] + sums[1] + sums[2], axis=1, keepdims=True) / total_features
        inverse = lax.rsqrt(mean + 1e-06)

        @pl.loop(0, both // tile)
        def _(t):
            cols = pl.ds(pl.multiple_of(t * tile, tile), tile)
            value = (
                own[j, chip, :, cols].astype(F32)
                + pair_recv[j, chip, :, cols].astype(F32)
                + cross_recv[j, :, cols].astype(F32)
            )
            rows[j, seq, :, cols] = (value * inverse).astype(BF16)

        row_copy(j).start()

    def stage_attend(j):
        row_copy(j).wait_recv()
        caption = image_caption[4 * seg + j]
        from_first = caption < caption_count
        live = caption_lengths[caption]
        mask = lax.broadcasted_iota(jnp.int32, (patches, slots), 1) < live
        for h in range(head_count):
            cols = slice(h * HEAD, (h + 1) * HEAD)
            vcols = slice(width + h * HEAD, width + (h + 1) * HEAD)
            scores = lax.dot_general(
                query_v[j, :, cols], jnp.where(from_first, rows[j, 0, :, cols], rows[j, 1, :, cols]),
                (((1,), (1,)), ((), ())), preferred_element_type=F32,
            ) * HEAD ** (-0.5)
            scores = jnp.where(mask, scores, -1e30)
            top = jnp.max(scores, axis=1, keepdims=True)
            expd = jnp.exp(scores - top)
            weights = (expd / jnp.sum(expd, axis=1, keepdims=True)).astype(BF16)
            attended[j, :, cols] = jnp.dot(
                weights,
                jnp.where(from_first, rows[j, 0, :, vcols], rows[j, 1, :, vcols]),
                preferred_element_type=F32,
            ).astype(BF16)

    def up_copy(n, j):
        return pltpu.make_async_remote_copy(
            src_ref=moving.at[n, j], dst_ref=moving.at[n, j],
            send_sem=z_ssem.at[n, j], recv_sem=z_rsem.at[n, j],
            device_id=device({"mp": lax.min(mp + 1, 3)}), device_id_type=MESH,
        )

    def down_copy(n, j):
        return pltpu.make_async_remote_copy(
            src_ref=moving.at[n, j], dst_ref=moving.at[n, j],
            send_sem=z_ssem.at[n, j], recv_sem=z_rsem.at[n, j],
            device_id=device({"mp": lax.max(mp - 1, 0)}), device_id_type=MESH,
        )

    def last_copy(n, j):
        return pltpu.make_async_remote_copy(
            src_ref=moving.at[n, j], dst_ref=from_right.at[j],
            send_sem=z_ssem.at[n, j], recv_sem=left_rsem.at[j],
            device_id=device({"mp": lax.max(mp - 1, 0)}), device_id_type=MESH,
        )

    def send_on(n, j):
        @pl.when(n > mp)
        def _():
            up_copy(n, j).start()

        @pl.when(n < mp - 1)
        def _():
            down_copy(n, j).start()

        @pl.when(n == mp - 1)
        def _():
            last_copy(n, j).start()

    def source_step(n, j):
        @pl.loop(0, width // tile)
        def _(t):
            cols = pl.ds(pl.multiple_of(t * tile, tile), tile)
            moving[n, j, :, cols] = jnp.dot(
                attended[j], out_w[n, :, cols], preferred_element_type=F32
            ).astype(BF16)

        send_on(n, j)

    def relay_step(n, j):
        up_copy(n, j).wait_recv()

        @pl.loop(0, width // tile)
        def _(t):
            cols = pl.ds(pl.multiple_of(t * tile, tile), tile)
            share = jnp.dot(attended[j], out_w[n, :, cols], preferred_element_type=F32)
            moving[n, j, :, cols] = (share + moving[n, j, :, cols].astype(F32)).astype(BF16)

        send_on(n, j)

    def final_step(j):
        @pl.when(mp > 0)
        def _():
            up_copy(mp, j).wait_recv()

        @pl.when(mp < 3)
        def _():
            last_copy(mp, j).wait_recv()

        @pl.loop(0, width // tile)
        def _(t):
            cols = pl.ds(pl.multiple_of(t * tile, tile), tile)
            share = jnp.dot(attended[j], out_w[mp, :, cols], preferred_element_type=F32)
            below = moving[mp, j, :, cols].astype(F32)
            above = from_right[j, :, cols].astype(F32)
            share = share + jnp.where(mp > 0, below, 0.0) + jnp.where(mp < 3, above, 0.0)
            result[j, :, cols] = (
                hidden_v[j, :, cols].astype(F32) + gate[j, :, cols] * share
            ).astype(BF16)

    is_end = (mp == 0) | (mp == 3)
    first = jnp.where(mp < 2, 3, 0)
    third = 1 + seq
    late = 2 - seq
    end_order = (first, third)

    def wait_send(n, j):
        up_copy(n, j).wait_send()

    @pl.loop(0, images + 4)
    def _(t):
        @pl.when(t < images)
        def _():
            stage_partial(t)

        @pl.when((t >= 1) & (t < images + 1))
        def _():
            stage_pair(t - 1)

        @pl.when((t >= 2) & (t < images + 2))
        def _():
            stage_rows(t - 2)

        @pl.when(t == images + 1)
        def _():
            w_copy(1).start()

        @pl.when((t >= 3) & (t < images + 3))
        def _():
            j = t - 3

            @pl.when(j == 0)
            def _():
                loads[3].wait()

            stage_attend(j)

            @pl.when(j == 0)
            def _():
                w_copy(0).wait_recv()
                w_forward(0).start()
                loads[4].wait()
                loads[5].wait()
                w_forward(0).wait_recv()

            @pl.when(is_end)
            def _():
                for n in end_order:
                    @pl.when(j >= 1)
                    def _():
                        wait_send(n, j - 1)

                    source_step(n, j)

        @pl.when((t >= 4) & jnp.logical_not(is_end))
        def _():
            j = t - 4
            relay_step(first, j)
            relay_step(3 - first, j)

            @pl.when(third != mp)
            def _():
                relay_step(third, j)

    w_copy(1).wait_recv()
    w_forward(1).start()
    w_forward(1).wait_recv()
    loads[6].wait()

    @pl.loop(0, images)
    def _(j):
        @pl.when(is_end)
        def _():
            @pl.when(j == 0)
            def _():
                for n in end_order:
                    wait_send(n, images - 1)

            @pl.when(j >= 1)
            def _():
                wait_send(late, j - 1)

            source_step(late, j)

        @pl.when(jnp.logical_not(is_end) & (late != mp))
        def _():
            relay_step(late, j)

        final_step(j)

    for step in range(2):
        w_copy(step).wait_send()
        w_forward(step).wait_send()

    @pl.loop(0, images)
    def _(j):
        pair_copy(j).wait_send()
        cross_copy(j).wait_send()
        row_copy(j).wait_send()

        @pl.when(jnp.logical_not(is_end))
        def _():
            wait_send(first, j)
            wait_send(3 - first, j)

            @pl.when(third != mp)
            def _():
                wait_send(third, j)

            @pl.when(late != mp)
            def _():
                wait_send(late, j)

    @pl.when(is_end)
    def _():
        wait_send(late, images - 1)


def fused_shards(
    captions,
    caption_lengths,
    image_caption,
    t5_gain,
    w_key,
    w_value,
    queries,
    hidden,
    out_gate,
    w_out,
):
    caption_count, slots, features = captions.shape
    images, patches, width = queries.shape
    packed = 2 * width + HEAD
    smem = pl.BlockSpec(memory_space=pltpu.SMEM)
    vmem = pl.BlockSpec(memory_space=pltpu.VMEM)
    hbm = pl.BlockSpec(memory_space=pl.ANY)
    dma = pltpu.SemaphoreType.DMA
    return pl.pallas_call(
        fused_kernel,
        out_shape=jax.ShapeDtypeStruct(queries.shape, BF16),
        in_specs=[smem, smem, vmem, vmem, hbm, hbm, hbm, hbm, hbm, hbm],
        out_specs=vmem,
        scratch_shapes=[
            pltpu.VMEM(captions.shape, BF16),
            pltpu.VMEM(w_key.shape, BF16),
            pltpu.VMEM(w_value.shape, BF16),
            pltpu.VMEM(queries.shape, BF16),
            pltpu.VMEM(hidden.shape, BF16),
            pltpu.VMEM((4, w_out.shape[0], width), BF16),
            pltpu.VMEM(captions.shape, BF16),
            pltpu.VMEM((caption_count, slots, HEAD), BF16),
            pltpu.VMEM((images, 2, slots, packed), BF16),
            pltpu.VMEM((images, 2, slots, packed), BF16),
            pltpu.VMEM((images, 2, slots, packed), BF16),
            pltpu.VMEM((images, slots, packed), BF16),
            pltpu.VMEM((images, 2, slots, 2 * width), BF16),
            pltpu.VMEM(queries.shape, BF16),
            pltpu.VMEM((4,) + queries.shape, BF16),
            pltpu.VMEM(queries.shape, BF16),
            dma((7,)),
            dma((images,)), dma((images,)),
            dma((images,)), dma((images,)),
            dma((images,)), dma((images,)),
            dma((2,)), dma((2,)), dma((2,)), dma((2,)),
            dma((4, images)), dma((4, images)), dma((images,)),
        ],
        compiler_params=pltpu.CompilerParams(
            collective_id=0, has_side_effects=True, vmem_limit_bytes=60 * 1024 * 1024
        ),
        cost_estimate=pl.CostEstimate(
            flops=20_000_000_000, bytes_accessed=20_000_000, transcendentals=1_100_000
        ),
    )(
        image_caption, caption_lengths, t5_gain.reshape(1, -1), out_gate.reshape(images, 1, width),
        captions, w_key, w_value, queries, hidden, w_out,
    )


def solution(mesh):
    in_specs = (
        P("seq", None, "segment"),
        P(),
        P(),
        P("segment"),
        P("segment", "mp"),
        P("segment", "mp"),
        P("segment", "seq", "mp"),
        P("segment", "seq", "mp"),
        P("segment", "mp"),
        P("mp", "seq"),
    )
    out_specs = P("segment", "seq", "mp")
    fused = (mesh.shape["segment"], mesh.shape["seq"], mesh.shape["mp"]) == (4, 2, 4)
    shards = fused_shards if fused else general_shards
    return jax.shard_map(shards, mesh=mesh, in_specs=in_specs, out_specs=out_specs, check_vma=False)
```

```python
import functools

import jax
import jax.numpy as jnp
from jax import lax
from jax.experimental import pallas as pl
from jax.experimental.pallas import tpu as pltpu
from jax.sharding import PartitionSpec as P

HEAD = 128
MESH = pl.DeviceIdType.MESH
BF16 = jnp.bfloat16
F32 = jnp.float32


def general_shards(
    captions,
    caption_lengths,
    image_caption,
    t5_gain,
    w_key,
    w_value,
    queries,
    hidden,
    out_gate,
    w_out,
):
    caption_count, caption_slots, feature_share = captions.shape
    image_count, patch_count, head_cols = queries.shape
    segment_count = lax.axis_size("segment")
    caption_values = captions.astype(jnp.float32)
    squares_total = lax.psum(jnp.sum(caption_values * caption_values, axis=2), "segment")
    inverse_rms = lax.rsqrt(squares_total / (feature_share * segment_count) + 1e-06)
    normed = (caption_values * inverse_rms[:, :, None] * t5_gain).astype(jnp.bfloat16)
    flattened = normed.reshape(caption_count * caption_slots, feature_share)
    key_partial = jnp.dot(flattened, w_key, preferred_element_type=jnp.float32)
    value_partial = jnp.dot(flattened, w_value, preferred_element_type=jnp.float32)
    first_image = lax.axis_index("segment") * image_count
    owner_ids = lax.dynamic_slice_in_dim(image_caption, first_image, image_count)
    stacked = jnp.concatenate([key_partial, value_partial], axis=1)
    column_share = lax.psum_scatter(
        stacked.astype(jnp.bfloat16), "segment", scatter_dimension=1, tiled=True
    ).astype(jnp.float32)
    piece_width = column_share.shape[1]
    column_share = column_share.astype(jnp.bfloat16).reshape(
        1, caption_count, caption_slots, piece_width
    )
    pieces = lax.all_gather(column_share, ("segment", "seq"), axis=0, tiled=True)
    pieces = pieces.reshape(segment_count, -1, caption_slots, piece_width)
    encoded = pieces.transpose(1, 2, 0, 3).reshape(
        pieces.shape[1], caption_slots, segment_count * piece_width
    )
    chosen = jnp.take(encoded, owner_ids, axis=0)
    live_lengths = jnp.take(caption_lengths, owner_ids)
    live_mask = jnp.arange(caption_slots, dtype=jnp.int32)[None, :] < live_lengths[:, None]
    head_count = head_cols // HEAD
    query_heads = queries.reshape(image_count, patch_count, head_count, HEAD)
    key_heads = chosen[:, :, :head_cols].reshape(image_count, caption_slots, head_count, HEAD)
    value_heads = chosen[:, :, head_cols:].reshape(image_count, caption_slots, head_count, HEAD)
    scores = jnp.einsum(
        "iphd,ikhd->ihpk", query_heads, key_heads, preferred_element_type=jnp.float32
    ) * HEAD ** (-0.5)
    scores = jnp.where(live_mask[:, None, None, :], scores, -1e30)
    weights = jax.nn.softmax(scores, axis=3).astype(jnp.bfloat16)
    attended = jnp.einsum(
        "ihpk,ikhd->iphd", weights, value_heads, preferred_element_type=jnp.float32
    )
    attended = attended.astype(jnp.bfloat16).reshape(image_count * patch_count, head_cols)
    partial_value = jnp.dot(
        attended,
        lax.all_gather(w_out, "seq", axis=1, tiled=True),
        preferred_element_type=jnp.float32,
    )
    mixed_heads = lax.psum_scatter(
        partial_value.astype(jnp.bfloat16), "mp", scatter_dimension=1, tiled=True
    ).astype(jnp.float32)
    result_rows = hidden.astype(jnp.float32) + out_gate[:, None, :] * mixed_heads.reshape(
        image_count, patch_count, head_cols
    )
    return result_rows.astype(jnp.bfloat16)


def fused_kernel(
    image_caption, caption_lengths, gain, gate, captions, w_key, w_value, queries, hidden, w_out,
    result,
    cap_raw, kv_w, query_v, out_w, scaled, squares,
    pair_send, pair_recv, own, cross_recv, rows, attended, moving, from_right, end_rows, end_w,
    local_sem, pair_ssem, pair_rsem, cross_ssem, cross_rsem, row_ssem, row_rsem,
    w_ssem, w_rsem, wf_ssem, wf_rsem, z_ssem, z_rsem, left_rsem,
    end_ssem, end_rsem, ew_ssem, ew_rsem, ewf_ssem, ewf_rsem,
):
    seg = lax.axis_index("segment")
    seq = lax.axis_index("seq")
    mp = lax.axis_index("mp")
    chip, core = seg // 2, seg % 2
    pair_id = {"segment": seg + 1 - 2 * core}
    cross_id = {"segment": (seg + 2) % 4}
    seq_id = {"seq": 1 - seq}
    caption_count, slots, features = cap_raw.shape
    images, patches, width = query_v.shape
    rounds = 2 * images
    head_count = width // HEAD
    half = out_w.shape[1] // 2
    total_features = 4 * features

    def device(ids):
        return {"segment": seg, "seq": seq, "mp": mp, **ids}

    loads = [
        pltpu.make_async_copy(captions, cap_raw, local_sem.at[0]),
        pltpu.make_async_copy(w_key, kv_w.at[0], local_sem.at[1]),
        pltpu.make_async_copy(w_value, kv_w.at[1], local_sem.at[2]),
        pltpu.make_async_copy(queries, query_v, local_sem.at[3]),
        pltpu.make_async_copy(
            w_out.at[:, pl.ds(0, width)], out_w.at[2 * seq], local_sem.at[4]
        ),
        pltpu.make_async_copy(
            w_out.at[:, pl.ds(width, width)], out_w.at[2 * seq + 1], local_sem.at[5]
        ),
    ]
    hidden_load = pltpu.make_async_copy(hidden, query_v, local_sem.at[6])
    for load in loads:
        load.start()

    barrier = pltpu.get_barrier_semaphore()
    for ids in (pair_id, cross_id, seq_id):
        pl.semaphore_signal(barrier, inc=1, device_id=device(ids), device_id_type=MESH)

    @pl.when(mp > 0)
    def _():
        pl.semaphore_signal(barrier, inc=1, device_id=device({"mp": mp - 1}), device_id_type=MESH)

    @pl.when(mp < 3)
    def _():
        pl.semaphore_signal(barrier, inc=1, device_id=device({"mp": mp + 1}), device_id_type=MESH)

    neighbours = 5 - (mp == 0).astype(jnp.int32) - (mp == 3).astype(jnp.int32)
    pl.semaphore_wait(barrier, neighbours)

    half_rows = pl.ds(pl.multiple_of(core * half, half), half)

    def w_copy(step):
        local_block = seq if step == 0 else 1 - seq
        block = 2 * seq + local_block
        return pltpu.make_async_remote_copy(
            src_ref=w_out.at[half_rows, pl.ds(pl.multiple_of(local_block * width, width), width)],
            dst_ref=out_w.at[block, half_rows],
            send_sem=w_ssem.at[step],
            recv_sem=w_rsem.at[step],
            device_id=device(seq_id),
            device_id_type=MESH,
        )

    def w_forward(step):
        other = 1 - seq
        block = 2 * other + (other if step == 0 else 1 - other)
        return pltpu.make_async_remote_copy(
            src_ref=out_w.at[block, half_rows],
            dst_ref=out_w.at[block, half_rows],
            send_sem=wf_ssem.at[step],
            recv_sem=wf_rsem.at[step],
            device_id=device(pair_id),
            device_id_type=MESH,
        )

    is_end = (mp == 0) | (mp == 3)
    first = jnp.where(mp < 2, 3, 0)
    third = 1 + seq
    late = 2 - seq
    inward = jnp.where(mp < 2, 1, 2)
    owns_first = (first // 2) == seq

    def end_w_direct(step):
        local_block = seq if step == 0 else 1 - seq
        return pltpu.make_async_remote_copy(
            src_ref=w_out.at[half_rows, pl.ds(pl.multiple_of(local_block * width, width), width)],
            dst_ref=end_w.at[step, half_rows],
            send_sem=ew_ssem.at[step], recv_sem=ew_rsem.at[step],
            device_id=device({"mp": inward}), device_id_type=MESH,
        )

    def end_w_received():
        return pltpu.make_async_remote_copy(
            src_ref=out_w.at[first, half_rows],
            dst_ref=end_w.at[0, half_rows],
            send_sem=ew_ssem.at[0], recv_sem=ew_rsem.at[0],
            device_id=device({"mp": inward}), device_id_type=MESH,
        )

    def end_w_forward(step):
        return pltpu.make_async_remote_copy(
            src_ref=end_w.at[step, half_rows],
            dst_ref=end_w.at[step, half_rows],
            send_sem=ewf_ssem.at[step], recv_sem=ewf_rsem.at[step],
            device_id=device(pair_id), device_id_type=MESH,
        )

    def end_copy(j):
        return pltpu.make_async_remote_copy(
            src_ref=attended.at[j], dst_ref=end_rows.at[j],
            send_sem=end_ssem.at[j], recv_sem=end_rsem.at[j],
            device_id=device({"mp": inward}), device_id_type=MESH,
        )

    w_copy(0).start()

    @pl.when(is_end)
    def _():
        @pl.when(owns_first)
        def _():
            end_w_direct(0).start()

        end_w_direct(1).start()

    loads[0].wait()

    @pl.loop(0, caption_count)
    def _(c):
        values = cap_raw[c].astype(F32)
        scaled[c] = (values * gain[...]).astype(BF16)
        square = values * values
        folded = square[:, :HEAD]
        for group in range(1, features // HEAD):
            folded = folded + square[:, group * HEAD : (group + 1) * HEAD]
        squares[c] = folded.astype(BF16)

    loads[1].wait()
    loads[2].wait()
    tile = 256

    def slot_partial(u, out_core, dst):
        ids = [image_caption[4 * (2 * x + out_core) + u // 2] % caption_count for x in range(2)]
        lhs = jnp.concatenate([scaled[i] for i in ids], axis=0)
        half_index = u % 2

        @pl.loop(0, width // tile)
        def _(t):
            cols = pl.ds(pl.multiple_of(t * tile, tile), tile)
            part = jnp.dot(lhs, kv_w[half_index, :, cols], preferred_element_type=F32).astype(BF16)
            for x in range(2):
                dst[u, x, :, cols] = part[x * slots : (x + 1) * slots]

        for x in range(2):
            dst[u, x, :, width:] = squares[ids[x]]

    def pair_copy(j):
        return pltpu.make_async_remote_copy(
            src_ref=pair_send.at[j], dst_ref=pair_recv.at[j],
            send_sem=pair_ssem.at[j], recv_sem=pair_rsem.at[j],
            device_id=device(pair_id), device_id_type=MESH,
        )

    def cross_copy(j):
        return pltpu.make_async_remote_copy(
            src_ref=own.at[j, 1 - chip], dst_ref=cross_recv.at[j],
            send_sem=cross_ssem.at[j], recv_sem=cross_rsem.at[j],
            device_id=device(cross_id), device_id_type=MESH,
        )

    def row_copy(j):
        return pltpu.make_async_remote_copy(
            src_ref=rows.at[j, seq], dst_ref=rows.at[j, seq],
            send_sem=row_ssem.at[j], recv_sem=row_rsem.at[j],
            device_id=device(seq_id), device_id_type=MESH,
        )

    def stage_partial(j):
        slot_partial(j, 1 - core, pair_send)
        pair_copy(j).start()
        slot_partial(j, core, own)

    def stage_pair(j):
        pair_copy(j).wait_recv()
        far = 1 - chip
        own[j, far] = (own[j, far].astype(F32) + pair_recv[j, far].astype(F32)).astype(BF16)
        cross_copy(j).start()

    def stage_rows(j):
        cross_copy(j).wait_recv()
        tail = pl.ds(width, HEAD)
        mean = jnp.sum(
            own[j, chip, :, tail].astype(F32)
            + pair_recv[j, chip, :, tail].astype(F32)
            + cross_recv[j, :, tail].astype(F32),
            axis=1, keepdims=True,
        ) / total_features
        inverse = lax.rsqrt(mean + 1e-06)

        @pl.loop(0, width // tile)
        def _(t):
            cols = pl.ds(pl.multiple_of(t * tile, tile), tile)
            value = (
                own[j, chip, :, cols].astype(F32)
                + pair_recv[j, chip, :, cols].astype(F32)
                + cross_recv[j, :, cols].astype(F32)
            )
            rows[j, seq, :, cols] = (value * inverse).astype(BF16)

        row_copy(j).start()

    def stage_attend(j):
        row_copy(2 * j).wait_recv()
        row_copy(2 * j + 1).wait_recv()
        caption = image_caption[4 * seg + j]
        from_first = caption < caption_count
        live = caption_lengths[caption]
        mask = lax.broadcasted_iota(jnp.int32, (patches, slots), 1) < live

        def picked(u, cols):
            return jnp.where(from_first, rows[u, 0, :, cols], rows[u, 1, :, cols])

        for h in range(head_count):
            cols = slice(h * HEAD, (h + 1) * HEAD)
            scores = lax.dot_general(
                query_v[j, :, cols], picked(2 * j, cols),
                (((1,), (1,)), ((), ())), preferred_element_type=F32,
            ) * HEAD ** (-0.5)
            scores = jnp.where(mask, scores, -1e30)
            top = jnp.max(scores, axis=1, keepdims=True)
            expd = jnp.exp(scores - top)
            weights = (expd / jnp.sum(expd, axis=1, keepdims=True)).astype(BF16)
            attended[j, :, cols] = jnp.dot(
                weights, picked(2 * j + 1, cols), preferred_element_type=F32
            ).astype(BF16)

    def up_copy(n, j):
        return pltpu.make_async_remote_copy(
            src_ref=moving.at[n, j], dst_ref=moving.at[n, j],
            send_sem=z_ssem.at[n, j], recv_sem=z_rsem.at[n, j],
            device_id=device({"mp": lax.min(mp + 1, 3)}), device_id_type=MESH,
        )

    def down_copy(n, j):
        return pltpu.make_async_remote_copy(
            src_ref=moving.at[n, j], dst_ref=moving.at[n, j],
            send_sem=z_ssem.at[n, j], recv_sem=z_rsem.at[n, j],
            device_id=device({"mp": lax.max(mp - 1, 0)}), device_id_type=MESH,
        )

    def last_copy(n, j):
        return pltpu.make_async_remote_copy(
            src_ref=moving.at[n, j], dst_ref=from_right.at[j],
            send_sem=z_ssem.at[n, j], recv_sem=left_rsem.at[j],
            device_id=device({"mp": lax.max(mp - 1, 0)}), device_id_type=MESH,
        )

    def send_on(n, j):
        @pl.when(n > mp)
        def _():
            up_copy(n, j).start()

        @pl.when(n < mp - 1)
        def _():
            down_copy(n, j).start()

        @pl.when(n == mp - 1)
        def _():
            last_copy(n, j).start()

    def source_step(n, j):
        @pl.loop(0, width // tile)
        def _(t):
            cols = pl.ds(pl.multiple_of(t * tile, tile), tile)
            moving[n, j, :, cols] = jnp.dot(
                attended[j], out_w[n, :, cols], preferred_element_type=F32
            ).astype(BF16)

        send_on(n, j)

    def relay_step(n, j):
        up_copy(n, j).wait_recv()

        @pl.loop(0, width // tile)
        def _(t):
            cols = pl.ds(pl.multiple_of(t * tile, tile), tile)
            share = jnp.dot(attended[j], out_w[n, :, cols], preferred_element_type=F32)
            moving[n, j, :, cols] = (share + moving[n, j, :, cols].astype(F32)).astype(BF16)

        send_on(n, j)

    def joint_step(n, step, j):
        @pl.loop(0, width // tile)
        def _(t):
            cols = pl.ds(pl.multiple_of(t * tile, tile), tile)
            share = jnp.dot(attended[j], out_w[n, :, cols], preferred_element_type=F32)
            share = share + jnp.dot(end_rows[j], end_w[step, :, cols], preferred_element_type=F32)
            moving[n, j, :, cols] = share.astype(BF16)

        send_on(n, j)

    from_below = (mp > 0) & jnp.logical_not((mp == 1) & (third == 1))
    from_above = (mp < 3) & jnp.logical_not((mp == 2) & (third == 2))
    has_end_term = jnp.logical_not(is_end) & (third == mp)

    def final_step(j):
        @pl.when(from_below)
        def _():
            up_copy(mp, j).wait_recv()

        @pl.when(from_above)
        def _():
            last_copy(mp, j).wait_recv()

        def finish(t, terms):
            cols = pl.ds(pl.multiple_of(t * tile, tile), tile)
            share = jnp.dot(attended[j], out_w[mp, :, cols], preferred_element_type=F32)
            for term in terms:
                share = share + term(cols)
            result[j, :, cols] = (
                query_v[j, :, cols].astype(F32) + gate[pl.ds(j, 1), cols] * share
            ).astype(BF16)

        def below(cols):
            return moving[mp, j, :, cols].astype(F32)

        def above(cols):
            return from_right[j, :, cols].astype(F32)

        def end_term(cols):
            return jnp.dot(end_rows[j], end_w[1, :, cols], preferred_element_type=F32)

        for condition, terms in (
            (mp == 0, (above,)),
            (mp == 3, (below,)),
            (has_end_term & (mp == 1), (above, end_term)),
            (has_end_term & (mp == 2), (below, end_term)),
            (jnp.logical_not(is_end) & (third != mp), (below, above)),
        ):
            @pl.when(condition)
            def _():
                pl.loop(0, width // tile)(lambda t: finish(t, terms))

    def wait_send(n, j):
        up_copy(n, j).wait_send()

    @pl.loop(0, rounds + 4)
    def _(u):
        @pl.when(u < rounds)
        def _():
            stage_partial(u)

        @pl.when((u >= 1) & (u < rounds + 1))
        def _():
            stage_pair(u - 1)

        @pl.when((u >= 2) & (u < rounds + 2))
        def _():
            stage_rows(u - 2)

        @pl.when(u == rounds + 1)
        def _():
            w_copy(1).start()

        @pl.when((u == 3) & is_end & jnp.logical_not(owns_first))
        def _():
            w_copy(0).wait_recv()
            end_w_received().start()

        @pl.when((u >= 4) & (u % 2 == 0))
        def _():
            j = (u - 4) // 2

            @pl.when(j == 0)
            def _():
                loads[3].wait()

            stage_attend(j)

            @pl.when(is_end)
            def _():
                end_copy(j).start()

        @pl.when((u >= 5) & (u % 2 == 1))
        def _():
            j = (u - 5) // 2

            @pl.when(j == 0)
            def _():
                @pl.when(jnp.logical_not(is_end & jnp.logical_not(owns_first)))
                def _():
                    w_copy(0).wait_recv()

                w_forward(0).start()
                loads[4].wait()
                loads[5].wait()

                @pl.when(jnp.logical_not(is_end))
                def _():
                    for step in range(2):
                        end_w_direct(step).wait_recv()
                        end_w_forward(step).start()

                    for step in range(2):
                        end_w_forward(step).wait_recv()

                w_forward(0).wait_recv()

            @pl.when(jnp.logical_not(is_end))
            def _():
                end_copy(j).wait_recv()
                joint_step(first, 0, j)

                @pl.when(third != mp)
                def _():
                    joint_step(third, 1, j)

                @pl.when(j >= 1)
                def _():
                    relay_step(3 - first, j - 1)

    hidden_load.start()

    @pl.when(jnp.logical_not(is_end))
    def _():
        relay_step(3 - first, images - 1)

    w_copy(1).wait_recv()
    w_forward(1).start()
    w_forward(1).wait_recv()
    hidden_load.wait()

    @pl.loop(0, images)
    def _(j):
        @pl.when(is_end)
        def _():
            @pl.when(j >= 2)
            def _():
                wait_send(late, j - 2)

            source_step(late, j)

        @pl.when(jnp.logical_not(is_end) & (late != mp))
        def _():
            relay_step(late, j)

        final_step(j)

    for step in range(2):
        w_copy(step).wait_send()
        w_forward(step).wait_send()

    @pl.loop(0, rounds)
    def _(u):
        pair_copy(u).wait_send()
        cross_copy(u).wait_send()
        row_copy(u).wait_send()

    @pl.when(is_end)
    def _():
        for step in range(2):
            end_w_direct(step).wait_send()

        for j in range(images):
            end_copy(j).wait_send()

        wait_send(late, images - 2)
        wait_send(late, images - 1)

    @pl.when(jnp.logical_not(is_end))
    def _():
        for step in range(2):
            end_w_forward(step).wait_send()

        @pl.loop(0, images)
        def _(j):
            wait_send(first, j)
            wait_send(3 - first, j)

            @pl.when(third != mp)
            def _():
                wait_send(third, j)

            @pl.when(late != mp)
            def _():
                wait_send(late, j)


def fused_shards(
    captions,
    caption_lengths,
    image_caption,
    t5_gain,
    w_key,
    w_value,
    queries,
    hidden,
    out_gate,
    w_out,
):
    caption_count, slots, features = captions.shape
    images, patches, width = queries.shape
    packed = width + HEAD
    rounds = 2 * images
    smem = pl.BlockSpec(memory_space=pltpu.SMEM)
    vmem = pl.BlockSpec(memory_space=pltpu.VMEM)
    hbm = pl.BlockSpec(memory_space=pl.ANY)
    dma = pltpu.SemaphoreType.DMA
    return pl.pallas_call(
        fused_kernel,
        out_shape=jax.ShapeDtypeStruct(queries.shape, BF16),
        in_specs=[smem, smem, vmem, vmem, hbm, hbm, hbm, hbm, hbm, hbm],
        out_specs=vmem,
        scratch_shapes=[
            pltpu.VMEM(captions.shape, BF16),
            pltpu.VMEM((2,) + w_key.shape, BF16),
            pltpu.VMEM(queries.shape, BF16),
            pltpu.VMEM((4, w_out.shape[0], width), BF16),
            pltpu.VMEM(captions.shape, BF16),
            pltpu.VMEM((caption_count, slots, HEAD), BF16),
            pltpu.VMEM((rounds, 2, slots, packed), BF16),
            pltpu.VMEM((rounds, 2, slots, packed), BF16),
            pltpu.VMEM((rounds, 2, slots, packed), BF16),
            pltpu.VMEM((rounds, slots, packed), BF16),
            pltpu.VMEM((rounds, 2, slots, width), BF16),
            pltpu.VMEM(queries.shape, BF16),
            pltpu.VMEM((4,) + queries.shape, BF16),
            pltpu.VMEM(queries.shape, BF16),
            pltpu.VMEM(queries.shape, BF16),
            pltpu.VMEM((2, w_out.shape[0], width), BF16),
            dma((7,)),
            dma((rounds,)), dma((rounds,)),
            dma((rounds,)), dma((rounds,)),
            dma((rounds,)), dma((rounds,)),
            dma((2,)), dma((2,)), dma((2,)), dma((2,)),
            dma((4, images)), dma((4, images)), dma((images,)),
            dma((images,)), dma((images,)),
            dma((2,)), dma((2,)), dma((2,)), dma((2,)),
        ],
        compiler_params=pltpu.CompilerParams(
            collective_id=0, has_side_effects=True, vmem_limit_bytes=60 * 1024 * 1024
        ),
        cost_estimate=pl.CostEstimate(
            flops=20_000_000_000, bytes_accessed=20_000_000, transcendentals=1_100_000
        ),
    )(
        image_caption, caption_lengths, t5_gain.reshape(1, -1), out_gate,
        captions, w_key, w_value, queries, hidden, w_out,
    )


def solution(mesh):
    in_specs = (
        P("seq", None, "segment"),
        P(),
        P(),
        P("segment"),
        P("segment", "mp"),
        P("segment", "mp"),
        P("segment", "seq", "mp"),
        P("segment", "seq", "mp"),
        P("segment", "mp"),
        P("mp", "seq"),
    )
    out_specs = P("segment", "seq", "mp")
    fused = (mesh.shape["segment"], mesh.shape["seq"], mesh.shape["mp"]) == (4, 2, 4)
    shards = fused_shards if fused else general_shards
    return jax.shard_map(shards, mesh=mesh, in_specs=in_specs, out_specs=out_specs, check_vma=False)
```

```python
import functools

import jax
import jax.numpy as jnp
from jax import lax
from jax.experimental import pallas as pl
from jax.experimental.pallas import tpu as pltpu
from jax.sharding import PartitionSpec as P

HEAD = 128
MESH = pl.DeviceIdType.MESH
BF16 = jnp.bfloat16
F32 = jnp.float32


def general_shards(
    captions,
    caption_lengths,
    image_caption,
    t5_gain,
    w_key,
    w_value,
    queries,
    hidden,
    out_gate,
    w_out,
):
    caption_count, caption_slots, feature_share = captions.shape
    image_count, patch_count, head_cols = queries.shape
    segment_count = lax.axis_size("segment")
    caption_values = captions.astype(jnp.float32)
    squares_total = lax.psum(jnp.sum(caption_values * caption_values, axis=2), "segment")
    inverse_rms = lax.rsqrt(squares_total / (feature_share * segment_count) + 1e-06)
    normed = (caption_values * inverse_rms[:, :, None] * t5_gain).astype(jnp.bfloat16)
    flattened = normed.reshape(caption_count * caption_slots, feature_share)
    key_partial = jnp.dot(flattened, w_key, preferred_element_type=jnp.float32)
    value_partial = jnp.dot(flattened, w_value, preferred_element_type=jnp.float32)
    first_image = lax.axis_index("segment") * image_count
    owner_ids = lax.dynamic_slice_in_dim(image_caption, first_image, image_count)
    stacked = jnp.concatenate([key_partial, value_partial], axis=1)
    column_share = lax.psum_scatter(
        stacked.astype(jnp.bfloat16), "segment", scatter_dimension=1, tiled=True
    ).astype(jnp.float32)
    piece_width = column_share.shape[1]
    column_share = column_share.astype(jnp.bfloat16).reshape(
        1, caption_count, caption_slots, piece_width
    )
    pieces = lax.all_gather(column_share, ("segment", "seq"), axis=0, tiled=True)
    pieces = pieces.reshape(segment_count, -1, caption_slots, piece_width)
    encoded = pieces.transpose(1, 2, 0, 3).reshape(
        pieces.shape[1], caption_slots, segment_count * piece_width
    )
    chosen = jnp.take(encoded, owner_ids, axis=0)
    live_lengths = jnp.take(caption_lengths, owner_ids)
    live_mask = jnp.arange(caption_slots, dtype=jnp.int32)[None, :] < live_lengths[:, None]
    head_count = head_cols // HEAD
    query_heads = queries.reshape(image_count, patch_count, head_count, HEAD)
    key_heads = chosen[:, :, :head_cols].reshape(image_count, caption_slots, head_count, HEAD)
    value_heads = chosen[:, :, head_cols:].reshape(image_count, caption_slots, head_count, HEAD)
    scores = jnp.einsum(
        "iphd,ikhd->ihpk", query_heads, key_heads, preferred_element_type=jnp.float32
    ) * HEAD ** (-0.5)
    scores = jnp.where(live_mask[:, None, None, :], scores, -1e30)
    weights = jax.nn.softmax(scores, axis=3).astype(jnp.bfloat16)
    attended = jnp.einsum(
        "ihpk,ikhd->iphd", weights, value_heads, preferred_element_type=jnp.float32
    )
    attended = attended.astype(jnp.bfloat16).reshape(image_count * patch_count, head_cols)
    partial_value = jnp.dot(
        attended,
        lax.all_gather(w_out, "seq", axis=1, tiled=True),
        preferred_element_type=jnp.float32,
    )
    mixed_heads = lax.psum_scatter(
        partial_value.astype(jnp.bfloat16), "mp", scatter_dimension=1, tiled=True
    ).astype(jnp.float32)
    result_rows = hidden.astype(jnp.float32) + out_gate[:, None, :] * mixed_heads.reshape(
        image_count, patch_count, head_cols
    )
    return result_rows.astype(jnp.bfloat16)


def fused_kernel(
    image_caption, caption_lengths, gain, gate, captions, w_key, w_value, queries, hidden, w_out,
    result,
    cap_raw, kv_w, query_v, out_w, scaled, squares,
    pair_send, pair_recv, own, cross_recv, rows, attended, moving, from_right, end_rows, end_w,
    local_sem, pair_ssem, pair_rsem, cross_ssem, cross_rsem, row_ssem, row_rsem,
    w_ssem, w_rsem, z_ssem, z_rsem, left_rsem,
    end_ssem, end_rsem, ew_ssem, ew_rsem, wx_ssem, wx_rsem, wp_ssem, wp_rsem,
):
    seg = lax.axis_index("segment")
    seq = lax.axis_index("seq")
    mp = lax.axis_index("mp")
    chip, core = seg // 2, seg % 2
    pair_id = {"segment": seg + 1 - 2 * core}
    cross_id = {"segment": (seg + 2) % 4}
    seq_id = {"seq": 1 - seq}
    caption_count, slots, features = cap_raw.shape
    images, patches, width = query_v.shape
    rounds = 2 * images
    head_count = width // HEAD
    quarter = out_w.shape[1] // 4
    total_features = 4 * features

    def device(ids):
        return {"segment": seg, "seq": seq, "mp": mp, **ids}

    loads = [
        pltpu.make_async_copy(captions, cap_raw, local_sem.at[0]),
        pltpu.make_async_copy(w_key, kv_w.at[0], local_sem.at[1]),
        pltpu.make_async_copy(w_value, kv_w.at[1], local_sem.at[2]),
        pltpu.make_async_copy(queries, query_v, local_sem.at[3]),
        pltpu.make_async_copy(
            w_out.at[:, pl.ds(0, width)], out_w.at[2 * seq], local_sem.at[4]
        ),
        pltpu.make_async_copy(
            w_out.at[:, pl.ds(width, width)], out_w.at[2 * seq + 1], local_sem.at[5]
        ),
    ]
    hidden_load = pltpu.make_async_copy(hidden, query_v, local_sem.at[6])
    for load in loads:
        load.start()

    barrier = pltpu.get_barrier_semaphore()
    for ids in (pair_id, cross_id, seq_id):
        pl.semaphore_signal(barrier, inc=1, device_id=device(ids), device_id_type=MESH)

    @pl.when(mp > 0)
    def _():
        pl.semaphore_signal(barrier, inc=1, device_id=device({"mp": mp - 1}), device_id_type=MESH)

    @pl.when(mp < 3)
    def _():
        pl.semaphore_signal(barrier, inc=1, device_id=device({"mp": mp + 1}), device_id_type=MESH)

    neighbours = 5 - (mp == 0).astype(jnp.int32) - (mp == 3).astype(jnp.int32)
    pl.semaphore_wait(barrier, neighbours)

    def quarter_of(owner):
        return pl.ds(pl.multiple_of(owner * quarter, quarter), quarter)

    near_rows = quarter_of(seg)
    far_rows = quarter_of((seg + 2) % 4)

    def w_copy(step):
        local_block = seq if step == 0 else 1 - seq
        block = 2 * seq + local_block
        return pltpu.make_async_remote_copy(
            src_ref=w_out.at[near_rows, pl.ds(pl.multiple_of(local_block * width, width), width)],
            dst_ref=out_w.at[block, near_rows],
            send_sem=w_ssem.at[step],
            recv_sem=w_rsem.at[step],
            device_id=device(seq_id),
            device_id_type=MESH,
        )

    is_end = (mp == 0) | (mp == 3)
    first = jnp.where(mp < 2, 3, 0)
    third = 1 + seq
    late = 2 - seq
    inward = jnp.where(mp < 2, 1, 2)
    owns_first = (first // 2) == seq

    def end_w_direct(step):
        local_block = seq if step == 0 else 1 - seq
        return pltpu.make_async_remote_copy(
            src_ref=w_out.at[near_rows, pl.ds(pl.multiple_of(local_block * width, width), width)],
            dst_ref=end_w.at[step, near_rows],
            send_sem=ew_ssem.at[step], recv_sem=ew_rsem.at[step],
            device_id=device({"mp": inward}), device_id_type=MESH,
        )

    def end_w_received():
        return pltpu.make_async_remote_copy(
            src_ref=out_w.at[first, near_rows],
            dst_ref=end_w.at[0, near_rows],
            send_sem=ew_ssem.at[0], recv_sem=ew_rsem.at[0],
            device_id=device({"mp": inward}), device_id_type=MESH,
        )

    other = 1 - seq
    blocks = (
        out_w.at[2 * other + other],
        out_w.at[2 * other + 1 - other],
        end_w.at[0],
        end_w.at[1],
    )

    def cross_spread(b):
        return pltpu.make_async_remote_copy(
            src_ref=blocks[b].at[near_rows], dst_ref=blocks[b].at[near_rows],
            send_sem=wx_ssem.at[b], recv_sem=wx_rsem.at[b],
            device_id=device(cross_id), device_id_type=MESH,
        )

    def pair_spread(b, i):
        part = far_rows if i else near_rows
        return pltpu.make_async_remote_copy(
            src_ref=blocks[b].at[part], dst_ref=blocks[b].at[part],
            send_sem=wp_ssem.at[b, i], recv_sem=wp_rsem.at[b, i],
            device_id=device(pair_id), device_id_type=MESH,
        )

    def spread_start(b):
        cross_spread(b).start()
        pair_spread(b, 0).start()

    def spread_far(b):
        cross_spread(b).wait_recv()
        pair_spread(b, 1).start()

    def spread_end(b):
        pair_spread(b, 0).wait_recv()
        pair_spread(b, 1).wait_recv()

    def spread_sent(b):
        cross_spread(b).wait_send()
        pair_spread(b, 0).wait_send()
        pair_spread(b, 1).wait_send()

    inner = jnp.logical_not(is_end)
    spreads_first = jnp.logical_not(is_end & jnp.logical_not(owns_first))

    def end_copy(j):
        return pltpu.make_async_remote_copy(
            src_ref=attended.at[j], dst_ref=end_rows.at[j],
            send_sem=end_ssem.at[j], recv_sem=end_rsem.at[j],
            device_id=device({"mp": inward}), device_id_type=MESH,
        )

    w_copy(0).start()

    @pl.when(is_end)
    def _():
        @pl.when(owns_first)
        def _():
            end_w_direct(0).start()

        end_w_direct(1).start()

    loads[0].wait()

    @pl.loop(0, caption_count)
    def _(c):
        values = cap_raw[c].astype(F32)
        scaled[c] = (values * gain[...]).astype(BF16)
        square = values * values
        folded = square[:, :HEAD]
        for group in range(1, features // HEAD):
            folded = folded + square[:, group * HEAD : (group + 1) * HEAD]
        squares[c] = folded.astype(BF16)

    loads[1].wait()
    loads[2].wait()
    tile = 256

    def slot_partial(u, out_core, dst):
        ids = [image_caption[4 * (2 * x + out_core) + u // 2] % caption_count for x in range(2)]
        lhs = jnp.concatenate([scaled[i] for i in ids], axis=0)
        half_index = u % 2

        @pl.loop(0, width // tile)
        def _(t):
            cols = pl.ds(pl.multiple_of(t * tile, tile), tile)
            part = jnp.dot(lhs, kv_w[half_index, :, cols], preferred_element_type=F32).astype(BF16)
            for x in range(2):
                dst[u, x, :, cols] = part[x * slots : (x + 1) * slots]

        for x in range(2):
            dst[u, x, :, width:] = squares[ids[x]]

    def pair_copy(j):
        return pltpu.make_async_remote_copy(
            src_ref=pair_send.at[j], dst_ref=pair_recv.at[j],
            send_sem=pair_ssem.at[j], recv_sem=pair_rsem.at[j],
            device_id=device(pair_id), device_id_type=MESH,
        )

    def cross_copy(j):
        return pltpu.make_async_remote_copy(
            src_ref=own.at[j, 1 - chip], dst_ref=cross_recv.at[j],
            send_sem=cross_ssem.at[j], recv_sem=cross_rsem.at[j],
            device_id=device(cross_id), device_id_type=MESH,
        )

    def row_copy(j):
        return pltpu.make_async_remote_copy(
            src_ref=rows.at[j, seq], dst_ref=rows.at[j, seq],
            send_sem=row_ssem.at[j], recv_sem=row_rsem.at[j],
            device_id=device(seq_id), device_id_type=MESH,
        )

    def stage_partial(j):
        slot_partial(j, 1 - core, pair_send)
        pair_copy(j).start()
        slot_partial(j, core, own)

    def stage_pair(j):
        pair_copy(j).wait_recv()
        far = 1 - chip
        own[j, far] = (own[j, far].astype(F32) + pair_recv[j, far].astype(F32)).astype(BF16)
        cross_copy(j).start()

    def stage_rows(j):
        cross_copy(j).wait_recv()
        tail = pl.ds(width, HEAD)
        mean = jnp.sum(
            own[j, chip, :, tail].astype(F32)
            + pair_recv[j, chip, :, tail].astype(F32)
            + cross_recv[j, :, tail].astype(F32),
            axis=1, keepdims=True,
        ) / total_features
        inverse = lax.rsqrt(mean + 1e-06)

        @pl.loop(0, width // tile)
        def _(t):
            cols = pl.ds(pl.multiple_of(t * tile, tile), tile)
            value = (
                own[j, chip, :, cols].astype(F32)
                + pair_recv[j, chip, :, cols].astype(F32)
                + cross_recv[j, :, cols].astype(F32)
            )
            rows[j, seq, :, cols] = (value * inverse).astype(BF16)

        row_copy(j).start()

    def stage_attend(j):
        row_copy(2 * j).wait_recv()
        row_copy(2 * j + 1).wait_recv()
        caption = image_caption[4 * seg + j]
        from_first = caption < caption_count
        live = caption_lengths[caption]
        mask = lax.broadcasted_iota(jnp.int32, (patches, slots), 1) < live

        def picked(u, cols):
            return jnp.where(from_first, rows[u, 0, :, cols], rows[u, 1, :, cols])

        for h in range(head_count):
            cols = slice(h * HEAD, (h + 1) * HEAD)
            scores = lax.dot_general(
                query_v[j, :, cols], picked(2 * j, cols),
                (((1,), (1,)), ((), ())), preferred_element_type=F32,
            ) * HEAD ** (-0.5)
            scores = jnp.where(mask, scores, -1e30)
            top = jnp.max(scores, axis=1, keepdims=True)
            expd = jnp.exp(scores - top)
            weights = (expd / jnp.sum(expd, axis=1, keepdims=True)).astype(BF16)
            attended[j, :, cols] = jnp.dot(
                weights, picked(2 * j + 1, cols), preferred_element_type=F32
            ).astype(BF16)

    def up_copy(n, j):
        return pltpu.make_async_remote_copy(
            src_ref=moving.at[n, j], dst_ref=moving.at[n, j],
            send_sem=z_ssem.at[n, j], recv_sem=z_rsem.at[n, j],
            device_id=device({"mp": lax.min(mp + 1, 3)}), device_id_type=MESH,
        )

    def down_copy(n, j):
        return pltpu.make_async_remote_copy(
            src_ref=moving.at[n, j], dst_ref=moving.at[n, j],
            send_sem=z_ssem.at[n, j], recv_sem=z_rsem.at[n, j],
            device_id=device({"mp": lax.max(mp - 1, 0)}), device_id_type=MESH,
        )

    def last_copy(n, j):
        return pltpu.make_async_remote_copy(
            src_ref=moving.at[n, j], dst_ref=from_right.at[j],
            send_sem=z_ssem.at[n, j], recv_sem=left_rsem.at[j],
            device_id=device({"mp": lax.max(mp - 1, 0)}), device_id_type=MESH,
        )

    def send_on(n, j):
        @pl.when(n > mp)
        def _():
            up_copy(n, j).start()

        @pl.when(n < mp - 1)
        def _():
            down_copy(n, j).start()

        @pl.when(n == mp - 1)
        def _():
            last_copy(n, j).start()

    def source_step(n, j):
        @pl.loop(0, width // tile)
        def _(t):
            cols = pl.ds(pl.multiple_of(t * tile, tile), tile)
            moving[n, j, :, cols] = jnp.dot(
                attended[j], out_w[n, :, cols], preferred_element_type=F32
            ).astype(BF16)

        send_on(n, j)

    def relay_step(n, j):
        up_copy(n, j).wait_recv()

        @pl.loop(0, width // tile)
        def _(t):
            cols = pl.ds(pl.multiple_of(t * tile, tile), tile)
            share = jnp.dot(attended[j], out_w[n, :, cols], preferred_element_type=F32)
            moving[n, j, :, cols] = (share + moving[n, j, :, cols].astype(F32)).astype(BF16)

        send_on(n, j)

    def joint_step(n, step, j):
        @pl.loop(0, width // tile)
        def _(t):
            cols = pl.ds(pl.multiple_of(t * tile, tile), tile)
            share = jnp.dot(attended[j], out_w[n, :, cols], preferred_element_type=F32)
            share = share + jnp.dot(end_rows[j], end_w[step, :, cols], preferred_element_type=F32)
            moving[n, j, :, cols] = share.astype(BF16)

        send_on(n, j)

    from_below = (mp > 0) & jnp.logical_not((mp == 1) & (third == 1))
    from_above = (mp < 3) & jnp.logical_not((mp == 2) & (third == 2))
    has_end_term = jnp.logical_not(is_end) & (third == mp)

    def final_step(j):
        @pl.when(from_below)
        def _():
            up_copy(mp, j).wait_recv()

        @pl.when(from_above)
        def _():
            last_copy(mp, j).wait_recv()

        def finish(t, terms):
            cols = pl.ds(pl.multiple_of(t * tile, tile), tile)
            share = jnp.dot(attended[j], out_w[mp, :, cols], preferred_element_type=F32)
            for term in terms:
                share = share + term(cols)
            result[j, :, cols] = (
                query_v[j, :, cols].astype(F32) + gate[pl.ds(j, 1), cols] * share
            ).astype(BF16)

        def below(cols):
            return moving[mp, j, :, cols].astype(F32)

        def above(cols):
            return from_right[j, :, cols].astype(F32)

        def end_term(cols):
            return jnp.dot(end_rows[j], end_w[1, :, cols], preferred_element_type=F32)

        for condition, terms in (
            (mp == 0, (above,)),
            (mp == 3, (below,)),
            (has_end_term & (mp == 1), (above, end_term)),
            (has_end_term & (mp == 2), (below, end_term)),
            (jnp.logical_not(is_end) & (third != mp), (below, above)),
        ):
            @pl.when(condition)
            def _():
                pl.loop(0, width // tile)(lambda t: finish(t, terms))

    def wait_send(n, j):
        up_copy(n, j).wait_send()

    @pl.loop(0, rounds + 6)
    def _(u):
        @pl.when(u < rounds)
        def _():
            stage_partial(u)

        @pl.when((u >= 1) & (u < rounds + 1))
        def _():
            stage_pair(u - 1)

        @pl.when((u >= 2) & (u < rounds + 2))
        def _():
            stage_rows(u - 2)

        @pl.when((u == 2) & is_end & jnp.logical_not(owns_first))
        def _():
            w_copy(0).wait_recv()
            end_w_received().start()

        @pl.when((u == 3) & spreads_first)
        def _():
            w_copy(0).wait_recv()
            spread_start(0)

        @pl.when((u >= 4) & (u % 2 == 0) & (u < rounds + 4))
        def _():
            j = (u - 4) // 2

            @pl.when(j == 0)
            def _():
                loads[3].wait()

            stage_attend(j)

            @pl.when(is_end)
            def _():
                end_copy(j).start()

        @pl.when(u == 4)
        def _():
            w_copy(1).start()

            @pl.when(inner)
            def _():
                end_w_direct(0).wait_recv()
                spread_start(2)

        @pl.when(u == 5)
        def _():
            @pl.when(spreads_first)
            def _():
                spread_far(0)

            @pl.when(inner)
            def _():
                end_w_direct(1).wait_recv()
                spread_start(3)

        @pl.when((u == 6) & inner)
        def _():
            spread_far(2)

        @pl.when(u == 8)
        def _():
            w_copy(1).wait_recv()
            spread_start(1)

        @pl.when(u == 10)
        def _():
            spread_far(1)

        @pl.when((u >= 7) & (u % 2 == 1))
        def _():
            j = (u - 7) // 2

            @pl.when(j == 0)
            def _():
                loads[4].wait()
                loads[5].wait()

                @pl.when(spreads_first)
                def _():
                    spread_end(0)

                @pl.when(inner)
                def _():
                    spread_far(3)
                    spread_end(2)

            @pl.when(inner)
            def _():
                end_copy(j).wait_recv()
                joint_step(first, 0, j)

                @pl.when(j == 0)
                def _():
                    spread_end(3)

                @pl.when(third != mp)
                def _():
                    joint_step(third, 1, j)

                @pl.when(j >= 1)
                def _():
                    relay_step(3 - first, j - 1)

    hidden_load.start()

    @pl.when(jnp.logical_not(is_end))
    def _():
        relay_step(3 - first, images - 1)

    spread_end(1)
    hidden_load.wait()

    @pl.loop(0, images)
    def _(j):
        @pl.when(is_end)
        def _():
            @pl.when(j >= 2)
            def _():
                wait_send(late, j - 2)

            source_step(late, j)

        @pl.when(jnp.logical_not(is_end) & (late != mp))
        def _():
            relay_step(late, j)

        final_step(j)

    for step in range(2):
        w_copy(step).wait_send()

    spread_sent(1)

    @pl.when(spreads_first)
    def _():
        spread_sent(0)

    @pl.loop(0, rounds)
    def _(u):
        pair_copy(u).wait_send()
        cross_copy(u).wait_send()
        row_copy(u).wait_send()

    @pl.when(is_end)
    def _():
        for step in range(2):
            end_w_direct(step).wait_send()

        for j in range(images):
            end_copy(j).wait_send()

        wait_send(late, images - 2)
        wait_send(late, images - 1)

    @pl.when(jnp.logical_not(is_end))
    def _():
        for step in range(2):
            spread_sent(2 + step)

        @pl.loop(0, images)
        def _(j):
            wait_send(first, j)
            wait_send(3 - first, j)

            @pl.when(third != mp)
            def _():
                wait_send(third, j)

            @pl.when(late != mp)
            def _():
                wait_send(late, j)


def fused_shards(
    captions,
    caption_lengths,
    image_caption,
    t5_gain,
    w_key,
    w_value,
    queries,
    hidden,
    out_gate,
    w_out,
):
    caption_count, slots, features = captions.shape
    images, patches, width = queries.shape
    packed = width + HEAD
    rounds = 2 * images
    smem = pl.BlockSpec(memory_space=pltpu.SMEM)
    vmem = pl.BlockSpec(memory_space=pltpu.VMEM)
    hbm = pl.BlockSpec(memory_space=pl.ANY)
    dma = pltpu.SemaphoreType.DMA
    return pl.pallas_call(
        fused_kernel,
        out_shape=jax.ShapeDtypeStruct(queries.shape, BF16),
        in_specs=[smem, smem, vmem, vmem, hbm, hbm, hbm, hbm, hbm, hbm],
        out_specs=vmem,
        scratch_shapes=[
            pltpu.VMEM(captions.shape, BF16),
            pltpu.VMEM((2,) + w_key.shape, BF16),
            pltpu.VMEM(queries.shape, BF16),
            pltpu.VMEM((4, w_out.shape[0], width), BF16),
            pltpu.VMEM(captions.shape, BF16),
            pltpu.VMEM((caption_count, slots, HEAD), BF16),
            pltpu.VMEM((rounds, 2, slots, packed), BF16),
            pltpu.VMEM((rounds, 2, slots, packed), BF16),
            pltpu.VMEM((rounds, 2, slots, packed), BF16),
            pltpu.VMEM((rounds, slots, packed), BF16),
            pltpu.VMEM((rounds, 2, slots, width), BF16),
            pltpu.VMEM(queries.shape, BF16),
            pltpu.VMEM((4,) + queries.shape, BF16),
            pltpu.VMEM(queries.shape, BF16),
            pltpu.VMEM(queries.shape, BF16),
            pltpu.VMEM((2, w_out.shape[0], width), BF16),
            dma((7,)),
            dma((rounds,)), dma((rounds,)),
            dma((rounds,)), dma((rounds,)),
            dma((rounds,)), dma((rounds,)),
            dma((2,)), dma((2,)),
            dma((4, images)), dma((4, images)), dma((images,)),
            dma((images,)), dma((images,)),
            dma((2,)), dma((2,)),
            dma((4,)), dma((4,)), dma((4, 2)), dma((4, 2)),
        ],
        compiler_params=pltpu.CompilerParams(
            collective_id=0, has_side_effects=True, vmem_limit_bytes=60 * 1024 * 1024
        ),
        cost_estimate=pl.CostEstimate(
            flops=20_000_000_000, bytes_accessed=20_000_000, transcendentals=1_100_000
        ),
    )(
        image_caption, caption_lengths, t5_gain.reshape(1, -1), out_gate,
        captions, w_key, w_value, queries, hidden, w_out,
    )


def solution(mesh):
    in_specs = (
        P("seq", None, "segment"),
        P(),
        P(),
        P("segment"),
        P("segment", "mp"),
        P("segment", "mp"),
        P("segment", "seq", "mp"),
        P("segment", "seq", "mp"),
        P("segment", "mp"),
        P("mp", "seq"),
    )
    out_specs = P("segment", "seq", "mp")
    fused = (mesh.shape["segment"], mesh.shape["seq"], mesh.shape["mp"]) == (4, 2, 4)
    shards = fused_shards if fused else general_shards
    return jax.shard_map(shards, mesh=mesh, in_specs=in_specs, out_specs=out_specs, check_vma=False)
```

```python
import functools

import jax
import jax.numpy as jnp
from jax import lax
from jax.experimental import pallas as pl
from jax.experimental.pallas import tpu as pltpu
from jax.sharding import PartitionSpec as P

HEAD = 128
MESH = pl.DeviceIdType.MESH
BF16 = jnp.bfloat16
F32 = jnp.float32


def general_shards(
    captions,
    caption_lengths,
    image_caption,
    t5_gain,
    w_key,
    w_value,
    queries,
    hidden,
    out_gate,
    w_out,
):
    caption_count, caption_slots, feature_share = captions.shape
    image_count, patch_count, head_cols = queries.shape
    segment_count = lax.axis_size("segment")
    caption_values = captions.astype(jnp.float32)
    squares_total = lax.psum(jnp.sum(caption_values * caption_values, axis=2), "segment")
    inverse_rms = lax.rsqrt(squares_total / (feature_share * segment_count) + 1e-06)
    normed = (caption_values * inverse_rms[:, :, None] * t5_gain).astype(jnp.bfloat16)
    flattened = normed.reshape(caption_count * caption_slots, feature_share)
    key_partial = jnp.dot(flattened, w_key, preferred_element_type=jnp.float32)
    value_partial = jnp.dot(flattened, w_value, preferred_element_type=jnp.float32)
    first_image = lax.axis_index("segment") * image_count
    owner_ids = lax.dynamic_slice_in_dim(image_caption, first_image, image_count)
    stacked = jnp.concatenate([key_partial, value_partial], axis=1)
    column_share = lax.psum_scatter(
        stacked.astype(jnp.bfloat16), "segment", scatter_dimension=1, tiled=True
    ).astype(jnp.float32)
    piece_width = column_share.shape[1]
    column_share = column_share.astype(jnp.bfloat16).reshape(
        1, caption_count, caption_slots, piece_width
    )
    pieces = lax.all_gather(column_share, ("segment", "seq"), axis=0, tiled=True)
    pieces = pieces.reshape(segment_count, -1, caption_slots, piece_width)
    encoded = pieces.transpose(1, 2, 0, 3).reshape(
        pieces.shape[1], caption_slots, segment_count * piece_width
    )
    chosen = jnp.take(encoded, owner_ids, axis=0)
    live_lengths = jnp.take(caption_lengths, owner_ids)
    live_mask = jnp.arange(caption_slots, dtype=jnp.int32)[None, :] < live_lengths[:, None]
    head_count = head_cols // HEAD
    query_heads = queries.reshape(image_count, patch_count, head_count, HEAD)
    key_heads = chosen[:, :, :head_cols].reshape(image_count, caption_slots, head_count, HEAD)
    value_heads = chosen[:, :, head_cols:].reshape(image_count, caption_slots, head_count, HEAD)
    scores = jnp.einsum(
        "iphd,ikhd->ihpk", query_heads, key_heads, preferred_element_type=jnp.float32
    ) * HEAD ** (-0.5)
    scores = jnp.where(live_mask[:, None, None, :], scores, -1e30)
    weights = jax.nn.softmax(scores, axis=3).astype(jnp.bfloat16)
    attended = jnp.einsum(
        "ihpk,ikhd->iphd", weights, value_heads, preferred_element_type=jnp.float32
    )
    attended = attended.astype(jnp.bfloat16).reshape(image_count * patch_count, head_cols)
    partial_value = jnp.dot(
        attended,
        lax.all_gather(w_out, "seq", axis=1, tiled=True),
        preferred_element_type=jnp.float32,
    )
    mixed_heads = lax.psum_scatter(
        partial_value.astype(jnp.bfloat16), "mp", scatter_dimension=1, tiled=True
    ).astype(jnp.float32)
    result_rows = hidden.astype(jnp.float32) + out_gate[:, None, :] * mixed_heads.reshape(
        image_count, patch_count, head_cols
    )
    return result_rows.astype(jnp.bfloat16)


def fused_kernel(
    image_caption, caption_lengths, gain, gate, captions, w_key, w_value, queries, hidden, w_out,
    result,
    cap_raw, kv_w, query_v, out_w, scaled, squares,
    pair_send, pair_recv, own, cross_recv, rows, attended, moving, from_right, end_rows, end_w,
    local_sem, pair_ssem, pair_rsem, cross_ssem, cross_rsem, row_ssem, row_rsem,
    w_ssem, w_rsem, z_ssem, z_rsem, left_rsem,
    end_ssem, end_rsem, ew_ssem, ew_rsem, wx_ssem, wx_rsem, wp_ssem, wp_rsem,
):
    seg = lax.axis_index("segment")
    seq = lax.axis_index("seq")
    mp = lax.axis_index("mp")
    chip, core = seg // 2, seg % 2
    pair_id = {"segment": seg + 1 - 2 * core}
    cross_id = {"segment": (seg + 2) % 4}
    seq_id = {"seq": 1 - seq}
    caption_count, slots, features = cap_raw.shape
    images, patches, width = query_v.shape
    rounds = 2 * images
    head_count = width // HEAD
    quarter = out_w.shape[1] // 4
    total_features = 4 * features

    def device(ids):
        return {"segment": seg, "seq": seq, "mp": mp, **ids}

    loads = [
        pltpu.make_async_copy(captions, cap_raw, local_sem.at[0]),
        pltpu.make_async_copy(w_key, kv_w.at[0], local_sem.at[1]),
        pltpu.make_async_copy(w_value, kv_w.at[1], local_sem.at[2]),
        pltpu.make_async_copy(queries, query_v, local_sem.at[3]),
        pltpu.make_async_copy(
            w_out.at[:, pl.ds(0, width)], out_w.at[2 * seq], local_sem.at[4]
        ),
        pltpu.make_async_copy(
            w_out.at[:, pl.ds(width, width)], out_w.at[2 * seq + 1], local_sem.at[5]
        ),
    ]
    hidden_load = pltpu.make_async_copy(hidden, query_v, local_sem.at[6])
    for load in loads:
        load.start()

    barrier = pltpu.get_barrier_semaphore()
    for ids in (pair_id, cross_id, seq_id):
        pl.semaphore_signal(barrier, inc=1, device_id=device(ids), device_id_type=MESH)

    @pl.when(mp > 0)
    def _():
        pl.semaphore_signal(barrier, inc=1, device_id=device({"mp": mp - 1}), device_id_type=MESH)

    @pl.when(mp < 3)
    def _():
        pl.semaphore_signal(barrier, inc=1, device_id=device({"mp": mp + 1}), device_id_type=MESH)

    neighbours = 5 - (mp == 0).astype(jnp.int32) - (mp == 3).astype(jnp.int32)
    pl.semaphore_wait(barrier, neighbours)

    def part_of(owner, size):
        return pl.ds(pl.multiple_of(owner * size, size), size)

    half_rows = part_of(core, 2 * quarter)
    near_rows = part_of(seg, quarter)
    far_rows = part_of((seg + 2) % 4, quarter)
    rows_of_step = (half_rows, near_rows)

    def w_copy(step):
        local_block = seq if step == 0 else 1 - seq
        block = 2 * seq + local_block
        return pltpu.make_async_remote_copy(
            src_ref=w_out.at[rows_of_step[step], pl.ds(pl.multiple_of(local_block * width, width), width)],
            dst_ref=out_w.at[block, rows_of_step[step]],
            send_sem=w_ssem.at[step],
            recv_sem=w_rsem.at[step],
            device_id=device(seq_id),
            device_id_type=MESH,
        )

    is_end = (mp == 0) | (mp == 3)
    first = jnp.where(mp < 2, 3, 0)
    third = 1 + seq
    late = 2 - seq
    inward = jnp.where(mp < 2, 1, 2)
    owns_first = (first // 2) == seq

    def end_w_direct(step):
        local_block = seq if step == 0 else 1 - seq
        return pltpu.make_async_remote_copy(
            src_ref=w_out.at[rows_of_step[step], pl.ds(pl.multiple_of(local_block * width, width), width)],
            dst_ref=end_w.at[step, rows_of_step[step]],
            send_sem=ew_ssem.at[step], recv_sem=ew_rsem.at[step],
            device_id=device({"mp": inward}), device_id_type=MESH,
        )

    def end_w_received():
        return pltpu.make_async_remote_copy(
            src_ref=out_w.at[first, half_rows],
            dst_ref=end_w.at[0, half_rows],
            send_sem=ew_ssem.at[0], recv_sem=ew_rsem.at[0],
            device_id=device({"mp": inward}), device_id_type=MESH,
        )

    other = 1 - seq
    blocks = (
        out_w.at[2 * other + other],
        out_w.at[2 * other + 1 - other],
        end_w.at[0],
        end_w.at[1],
    )

    def cross_spread(b):
        return pltpu.make_async_remote_copy(
            src_ref=blocks[b].at[near_rows], dst_ref=blocks[b].at[near_rows],
            send_sem=wx_ssem.at[b], recv_sem=wx_rsem.at[b],
            device_id=device(cross_id), device_id_type=MESH,
        )

    def pair_spread(b, i):
        part = far_rows if i else (near_rows if b % 2 else half_rows)
        return pltpu.make_async_remote_copy(
            src_ref=blocks[b].at[part], dst_ref=blocks[b].at[part],
            send_sem=wp_ssem.at[b, i], recv_sem=wp_rsem.at[b, i],
            device_id=device(pair_id), device_id_type=MESH,
        )

    def spread_start(b):
        if b % 2:
            cross_spread(b).start()
        pair_spread(b, 0).start()

    def spread_far(b):
        cross_spread(b).wait_recv()
        pair_spread(b, 1).start()

    def spread_end(b):
        pair_spread(b, 0).wait_recv()
        if b % 2:
            pair_spread(b, 1).wait_recv()

    def spread_sent(b):
        pair_spread(b, 0).wait_send()
        if b % 2:
            cross_spread(b).wait_send()
            pair_spread(b, 1).wait_send()

    inner = jnp.logical_not(is_end)
    spreads_first = jnp.logical_not(is_end & jnp.logical_not(owns_first))

    def end_copy(j):
        return pltpu.make_async_remote_copy(
            src_ref=attended.at[j], dst_ref=end_rows.at[j],
            send_sem=end_ssem.at[j], recv_sem=end_rsem.at[j],
            device_id=device({"mp": inward}), device_id_type=MESH,
        )

    w_copy(0).start()

    @pl.when(is_end)
    def _():
        @pl.when(owns_first)
        def _():
            end_w_direct(0).start()

        end_w_direct(1).start()

    loads[0].wait()

    @pl.loop(0, caption_count)
    def _(c):
        values = cap_raw[c].astype(F32)
        scaled[c] = (values * gain[...]).astype(BF16)
        square = values * values
        folded = square[:, :HEAD]
        for group in range(1, features // HEAD):
            folded = folded + square[:, group * HEAD : (group + 1) * HEAD]
        squares[c] = folded.astype(BF16)

    loads[1].wait()
    loads[2].wait()
    tile = 256

    def slot_partial(u, out_core, dst):
        ids = [image_caption[4 * (2 * x + out_core) + u // 2] % caption_count for x in range(2)]
        lhs = jnp.concatenate([scaled[i] for i in ids], axis=0)
        half_index = u % 2

        @pl.loop(0, width // tile)
        def _(t):
            cols = pl.ds(pl.multiple_of(t * tile, tile), tile)
            part = jnp.dot(lhs, kv_w[half_index, :, cols], preferred_element_type=F32).astype(BF16)
            for x in range(2):
                dst[u, x, :, cols] = part[x * slots : (x + 1) * slots]

        for x in range(2):
            dst[u, x, :, width:] = squares[ids[x]]

    def pair_copy(j):
        return pltpu.make_async_remote_copy(
            src_ref=pair_send.at[j], dst_ref=pair_recv.at[j],
            send_sem=pair_ssem.at[j], recv_sem=pair_rsem.at[j],
            device_id=device(pair_id), device_id_type=MESH,
        )

    def cross_copy(j):
        return pltpu.make_async_remote_copy(
            src_ref=own.at[j, 1 - chip], dst_ref=cross_recv.at[j],
            send_sem=cross_ssem.at[j], recv_sem=cross_rsem.at[j],
            device_id=device(cross_id), device_id_type=MESH,
        )

    def row_copy(j):
        return pltpu.make_async_remote_copy(
            src_ref=rows.at[j, seq], dst_ref=rows.at[j, seq],
            send_sem=row_ssem.at[j], recv_sem=row_rsem.at[j],
            device_id=device(seq_id), device_id_type=MESH,
        )

    def stage_partial(j):
        slot_partial(j, 1 - core, pair_send)
        pair_copy(j).start()
        slot_partial(j, core, own)

    def stage_pair(j):
        pair_copy(j).wait_recv()
        far = 1 - chip
        own[j, far] = (own[j, far].astype(F32) + pair_recv[j, far].astype(F32)).astype(BF16)
        cross_copy(j).start()

    def stage_rows(j):
        cross_copy(j).wait_recv()
        tail = pl.ds(width, HEAD)
        mean = jnp.sum(
            own[j, chip, :, tail].astype(F32)
            + pair_recv[j, chip, :, tail].astype(F32)
            + cross_recv[j, :, tail].astype(F32),
            axis=1, keepdims=True,
        ) / total_features
        inverse = lax.rsqrt(mean + 1e-06)

        @pl.loop(0, width // tile)
        def _(t):
            cols = pl.ds(pl.multiple_of(t * tile, tile), tile)
            value = (
                own[j, chip, :, cols].astype(F32)
                + pair_recv[j, chip, :, cols].astype(F32)
                + cross_recv[j, :, cols].astype(F32)
            )
            rows[j, seq, :, cols] = (value * inverse).astype(BF16)

        row_copy(j).start()

    def stage_attend(j):
        row_copy(2 * j).wait_recv()
        row_copy(2 * j + 1).wait_recv()
        caption = image_caption[4 * seg + j]
        from_first = caption < caption_count
        live = caption_lengths[caption]
        mask = lax.broadcasted_iota(jnp.int32, (patches, slots), 1) < live

        def picked(u, cols):
            return jnp.where(from_first, rows[u, 0, :, cols], rows[u, 1, :, cols])

        for h in range(head_count):
            cols = slice(h * HEAD, (h + 1) * HEAD)
            scores = lax.dot_general(
                query_v[j, :, cols], picked(2 * j, cols),
                (((1,), (1,)), ((), ())), preferred_element_type=F32,
            ) * HEAD ** (-0.5)
            scores = jnp.where(mask, scores, -1e30)
            top = jnp.max(scores, axis=1, keepdims=True)
            expd = jnp.exp(scores - top)
            weights = (expd / jnp.sum(expd, axis=1, keepdims=True)).astype(BF16)
            attended[j, :, cols] = jnp.dot(
                weights, picked(2 * j + 1, cols), preferred_element_type=F32
            ).astype(BF16)

    def up_copy(n, j):
        return pltpu.make_async_remote_copy(
            src_ref=moving.at[n, j], dst_ref=moving.at[n, j],
            send_sem=z_ssem.at[n, j], recv_sem=z_rsem.at[n, j],
            device_id=device({"mp": lax.min(mp + 1, 3)}), device_id_type=MESH,
        )

    def down_copy(n, j):
        return pltpu.make_async_remote_copy(
            src_ref=moving.at[n, j], dst_ref=moving.at[n, j],
            send_sem=z_ssem.at[n, j], recv_sem=z_rsem.at[n, j],
            device_id=device({"mp": lax.max(mp - 1, 0)}), device_id_type=MESH,
        )

    def last_copy(n, j):
        return pltpu.make_async_remote_copy(
            src_ref=moving.at[n, j], dst_ref=from_right.at[j],
            send_sem=z_ssem.at[n, j], recv_sem=left_rsem.at[j],
            device_id=device({"mp": lax.max(mp - 1, 0)}), device_id_type=MESH,
        )

    def send_on(n, j):
        @pl.when(n > mp)
        def _():
            up_copy(n, j).start()

        @pl.when(n < mp - 1)
        def _():
            down_copy(n, j).start()

        @pl.when(n == mp - 1)
        def _():
            last_copy(n, j).start()

    def source_step(n, j):
        @pl.loop(0, width // tile)
        def _(t):
            cols = pl.ds(pl.multiple_of(t * tile, tile), tile)
            moving[n, j, :, cols] = jnp.dot(
                attended[j], out_w[n, :, cols], preferred_element_type=F32
            ).astype(BF16)

        send_on(n, j)

    def relay_step(n, j):
        up_copy(n, j).wait_recv()

        @pl.loop(0, width // tile)
        def _(t):
            cols = pl.ds(pl.multiple_of(t * tile, tile), tile)
            share = jnp.dot(attended[j], out_w[n, :, cols], preferred_element_type=F32)
            moving[n, j, :, cols] = (share + moving[n, j, :, cols].astype(F32)).astype(BF16)

        send_on(n, j)

    def joint_step(n, step, j):
        @pl.loop(0, width // tile)
        def _(t):
            cols = pl.ds(pl.multiple_of(t * tile, tile), tile)
            share = jnp.dot(attended[j], out_w[n, :, cols], preferred_element_type=F32)
            share = share + jnp.dot(end_rows[j], end_w[step, :, cols], preferred_element_type=F32)
            moving[n, j, :, cols] = share.astype(BF16)

        send_on(n, j)

    from_below = (mp > 0) & jnp.logical_not((mp == 1) & (third == 1))
    from_above = (mp < 3) & jnp.logical_not((mp == 2) & (third == 2))
    has_end_term = jnp.logical_not(is_end) & (third == mp)

    def final_step(j):
        @pl.when(from_below)
        def _():
            up_copy(mp, j).wait_recv()

        @pl.when(from_above)
        def _():
            last_copy(mp, j).wait_recv()

        def finish(t, terms):
            cols = pl.ds(pl.multiple_of(t * tile, tile), tile)
            share = jnp.dot(attended[j], out_w[mp, :, cols], preferred_element_type=F32)
            for term in terms:
                share = share + term(cols)
            result[j, :, cols] = (
                query_v[j, :, cols].astype(F32) + gate[pl.ds(j, 1), cols] * share
            ).astype(BF16)

        def below(cols):
            return moving[mp, j, :, cols].astype(F32)

        def above(cols):
            return from_right[j, :, cols].astype(F32)

        def end_term(cols):
            return jnp.dot(end_rows[j], end_w[1, :, cols], preferred_element_type=F32)

        for condition, terms in (
            (mp == 0, (above,)),
            (mp == 3, (below,)),
            (has_end_term & (mp == 1), (above, end_term)),
            (has_end_term & (mp == 2), (below, end_term)),
            (jnp.logical_not(is_end) & (third != mp), (below, above)),
        ):
            @pl.when(condition)
            def _():
                pl.loop(0, width // tile)(lambda t: finish(t, terms))

    def wait_send(n, j):
        up_copy(n, j).wait_send()

    @pl.loop(0, rounds + 4)
    def _(u):
        @pl.when(u < rounds)
        def _():
            stage_partial(u)

        @pl.when((u >= 1) & (u < rounds + 1))
        def _():
            stage_pair(u - 1)

        @pl.when((u >= 2) & (u < rounds + 2))
        def _():
            stage_rows(u - 2)

        @pl.when((u == 3) & is_end & jnp.logical_not(owns_first))
        def _():
            w_copy(0).wait_recv()
            end_w_received().start()

        @pl.when((u >= 4) & (u % 2 == 0))
        def _():
            j = (u - 4) // 2

            @pl.when(j == 0)
            def _():
                loads[3].wait()

            stage_attend(j)

            @pl.when(is_end)
            def _():
                end_copy(j).start()

        @pl.when(u == 4)
        def _():
            @pl.when(spreads_first)
            def _():
                w_copy(0).wait_recv()
                spread_start(0)

            @pl.when(inner)
            def _():
                end_w_direct(1).wait_recv()
                spread_start(3)

        @pl.when(u == 8)
        def _():
            w_copy(1).wait_recv()
            spread_start(1)

        @pl.when(u == 10)
        def _():
            spread_far(1)

        @pl.when(u == 5)
        def _():
            w_copy(1).start()
            loads[4].wait()
            loads[5].wait()

            @pl.when(spreads_first)
            def _():
                spread_end(0)

            @pl.when(inner)
            def _():
                spread_far(3)
                end_w_direct(0).wait_recv()
                spread_start(2)
                spread_end(2)

        @pl.when((u >= 5) & (u % 2 == 1) & inner)
        def _():
            j = (u - 5) // 2
            end_copy(j).wait_recv()
            joint_step(first, 0, j)

            @pl.when(j == 0)
            def _():
                spread_end(3)

            @pl.when(third != mp)
            def _():
                joint_step(third, 1, j)

            @pl.when((j >= 1) & (j < images - 1))
            def _():
                relay_step(3 - first, j - 1)

    hidden_load.start()

    spread_end(1)

    @pl.when(is_end)
    def _():
        @pl.loop(0, images)
        def _(j):
            @pl.when(j >= 2)
            def _():
                wait_send(late, j - 2)

            source_step(late, j)

    @pl.when(inner)
    def _():
        @pl.loop(0, images + 2)
        def _(t):
            half_count = images // 2
            outward = (t == half_count) | (t == images + 1)
            late_j = t - (t > half_count).astype(jnp.int32)

            @pl.when(outward)
            def _():
                relay_step(3 - first, images - 2 + (t > half_count).astype(jnp.int32))

            @pl.when(jnp.logical_not(outward) & (late != mp))
            def _():
                relay_step(late, late_j)

    hidden_load.wait()

    @pl.loop(0, images)
    def _(j):
        final_step(j)

    for step in range(2):
        w_copy(step).wait_send()

    spread_sent(1)

    @pl.when(spreads_first)
    def _():
        spread_sent(0)

    @pl.loop(0, rounds)
    def _(u):
        pair_copy(u).wait_send()
        cross_copy(u).wait_send()
        row_copy(u).wait_send()

    @pl.when(is_end)
    def _():
        for step in range(2):
            end_w_direct(step).wait_send()

        for j in range(images):
            end_copy(j).wait_send()

        wait_send(late, images - 2)
        wait_send(late, images - 1)

    @pl.when(jnp.logical_not(is_end))
    def _():
        for step in range(2):
            spread_sent(2 + step)

        @pl.loop(0, images)
        def _(j):
            wait_send(first, j)
            wait_send(3 - first, j)

            @pl.when(third != mp)
            def _():
                wait_send(third, j)

            @pl.when(late != mp)
            def _():
                wait_send(late, j)


def fused_shards(
    captions,
    caption_lengths,
    image_caption,
    t5_gain,
    w_key,
    w_value,
    queries,
    hidden,
    out_gate,
    w_out,
):
    caption_count, slots, features = captions.shape
    images, patches, width = queries.shape
    packed = width + HEAD
    rounds = 2 * images
    smem = pl.BlockSpec(memory_space=pltpu.SMEM)
    vmem = pl.BlockSpec(memory_space=pltpu.VMEM)
    hbm = pl.BlockSpec(memory_space=pl.ANY)
    dma = pltpu.SemaphoreType.DMA
    return pl.pallas_call(
        fused_kernel,
        out_shape=jax.ShapeDtypeStruct(queries.shape, BF16),
        in_specs=[smem, smem, vmem, vmem, hbm, hbm, hbm, hbm, hbm, hbm],
        out_specs=vmem,
        scratch_shapes=[
            pltpu.VMEM(captions.shape, BF16),
            pltpu.VMEM((2,) + w_key.shape, BF16),
            pltpu.VMEM(queries.shape, BF16),
            pltpu.VMEM((4, w_out.shape[0], width), BF16),
            pltpu.VMEM(captions.shape, BF16),
            pltpu.VMEM((caption_count, slots, HEAD), BF16),
            pltpu.VMEM((rounds, 2, slots, packed), BF16),
            pltpu.VMEM((rounds, 2, slots, packed), BF16),
            pltpu.VMEM((rounds, 2, slots, packed), BF16),
            pltpu.VMEM((rounds, slots, packed), BF16),
            pltpu.VMEM((rounds, 2, slots, width), BF16),
            pltpu.VMEM(queries.shape, BF16),
            pltpu.VMEM((4,) + queries.shape, BF16),
            pltpu.VMEM(queries.shape, BF16),
            pltpu.VMEM(queries.shape, BF16),
            pltpu.VMEM((2, w_out.shape[0], width), BF16),
            dma((7,)),
            dma((rounds,)), dma((rounds,)),
            dma((rounds,)), dma((rounds,)),
            dma((rounds,)), dma((rounds,)),
            dma((2,)), dma((2,)),
            dma((4, images)), dma((4, images)), dma((images,)),
            dma((images,)), dma((images,)),
            dma((2,)), dma((2,)),
            dma((4,)), dma((4,)), dma((4, 2)), dma((4, 2)),
        ],
        compiler_params=pltpu.CompilerParams(
            collective_id=0, has_side_effects=True, vmem_limit_bytes=60 * 1024 * 1024
        ),
        cost_estimate=pl.CostEstimate(
            flops=20_000_000_000, bytes_accessed=20_000_000, transcendentals=1_100_000
        ),
    )(
        image_caption, caption_lengths, t5_gain.reshape(1, -1), out_gate,
        captions, w_key, w_value, queries, hidden, w_out,
    )


def solution(mesh):
    in_specs = (
        P("seq", None, "segment"),
        P(),
        P(),
        P("segment"),
        P("segment", "mp"),
        P("segment", "mp"),
        P("segment", "seq", "mp"),
        P("segment", "seq", "mp"),
        P("segment", "mp"),
        P("mp", "seq"),
    )
    out_specs = P("segment", "seq", "mp")
    fused = (mesh.shape["segment"], mesh.shape["seq"], mesh.shape["mp"]) == (4, 2, 4)
    shards = fused_shards if fused else general_shards
    return jax.shard_map(shards, mesh=mesh, in_specs=in_specs, out_specs=out_specs, check_vma=False)
```

```python
import functools

import jax
import jax.numpy as jnp
from jax import lax
from jax.experimental import pallas as pl
from jax.experimental.pallas import tpu as pltpu
from jax.sharding import PartitionSpec as P

HEAD = 128
MESH = pl.DeviceIdType.MESH
BF16 = jnp.bfloat16
F32 = jnp.float32


def general_shards(
    captions,
    caption_lengths,
    image_caption,
    t5_gain,
    w_key,
    w_value,
    queries,
    hidden,
    out_gate,
    w_out,
):
    caption_count, caption_slots, feature_share = captions.shape
    image_count, patch_count, head_cols = queries.shape
    segment_count = lax.axis_size("segment")
    caption_values = captions.astype(jnp.float32)
    squares_total = lax.psum(jnp.sum(caption_values * caption_values, axis=2), "segment")
    inverse_rms = lax.rsqrt(squares_total / (feature_share * segment_count) + 1e-06)
    normed = (caption_values * inverse_rms[:, :, None] * t5_gain).astype(jnp.bfloat16)
    flattened = normed.reshape(caption_count * caption_slots, feature_share)
    key_partial = jnp.dot(flattened, w_key, preferred_element_type=jnp.float32)
    value_partial = jnp.dot(flattened, w_value, preferred_element_type=jnp.float32)
    first_image = lax.axis_index("segment") * image_count
    owner_ids = lax.dynamic_slice_in_dim(image_caption, first_image, image_count)
    stacked = jnp.concatenate([key_partial, value_partial], axis=1)
    column_share = lax.psum_scatter(
        stacked.astype(jnp.bfloat16), "segment", scatter_dimension=1, tiled=True
    ).astype(jnp.float32)
    piece_width = column_share.shape[1]
    column_share = column_share.astype(jnp.bfloat16).reshape(
        1, caption_count, caption_slots, piece_width
    )
    pieces = lax.all_gather(column_share, ("segment", "seq"), axis=0, tiled=True)
    pieces = pieces.reshape(segment_count, -1, caption_slots, piece_width)
    encoded = pieces.transpose(1, 2, 0, 3).reshape(
        pieces.shape[1], caption_slots, segment_count * piece_width
    )
    chosen = jnp.take(encoded, owner_ids, axis=0)
    live_lengths = jnp.take(caption_lengths, owner_ids)
    live_mask = jnp.arange(caption_slots, dtype=jnp.int32)[None, :] < live_lengths[:, None]
    head_count = head_cols // HEAD
    query_heads = queries.reshape(image_count, patch_count, head_count, HEAD)
    key_heads = chosen[:, :, :head_cols].reshape(image_count, caption_slots, head_count, HEAD)
    value_heads = chosen[:, :, head_cols:].reshape(image_count, caption_slots, head_count, HEAD)
    scores = jnp.einsum(
        "iphd,ikhd->ihpk", query_heads, key_heads, preferred_element_type=jnp.float32
    ) * HEAD ** (-0.5)
    scores = jnp.where(live_mask[:, None, None, :], scores, -1e30)
    weights = jax.nn.softmax(scores, axis=3).astype(jnp.bfloat16)
    attended = jnp.einsum(
        "ihpk,ikhd->iphd", weights, value_heads, preferred_element_type=jnp.float32
    )
    attended = attended.astype(jnp.bfloat16).reshape(image_count * patch_count, head_cols)
    partial_value = jnp.dot(
        attended,
        lax.all_gather(w_out, "seq", axis=1, tiled=True),
        preferred_element_type=jnp.float32,
    )
    mixed_heads = lax.psum_scatter(
        partial_value.astype(jnp.bfloat16), "mp", scatter_dimension=1, tiled=True
    ).astype(jnp.float32)
    result_rows = hidden.astype(jnp.float32) + out_gate[:, None, :] * mixed_heads.reshape(
        image_count, patch_count, head_cols
    )
    return result_rows.astype(jnp.bfloat16)


def fused_kernel(
    image_caption, caption_lengths, gain, gate, captions, w_key, w_value, queries, hidden, w_out,
    result,
    cap_raw, kv_w, query_v, out_w, scaled, squares,
    pair_send, pair_recv, own, cross_recv, rows, attended, moving, from_right, end_rows, end_w,
    local_sem, pair_ssem, pair_rsem, cross_ssem, cross_rsem, row_ssem, row_rsem,
    w_ssem, w_rsem, z_ssem, z_rsem, left_rsem,
    end_ssem, end_rsem, ew_ssem, ew_rsem, wx_ssem, wx_rsem, wp_ssem, wp_rsem,
):
    seg = lax.axis_index("segment")
    seq = lax.axis_index("seq")
    mp = lax.axis_index("mp")
    chip, core = seg // 2, seg % 2
    pair_id = {"segment": seg + 1 - 2 * core}
    cross_id = {"segment": (seg + 2) % 4}
    seq_id = {"seq": 1 - seq}
    caption_count, slots, features = cap_raw.shape
    images, patches, width = query_v.shape
    rounds = 2 * images
    head_count = width // HEAD
    quarter = out_w.shape[1] // 4
    total_features = 4 * features

    def device(ids):
        return {"segment": seg, "seq": seq, "mp": mp, **ids}

    loads = [
        pltpu.make_async_copy(captions, cap_raw, local_sem.at[0]),
        pltpu.make_async_copy(w_key, kv_w.at[0], local_sem.at[1]),
        pltpu.make_async_copy(w_value, kv_w.at[1], local_sem.at[2]),
        pltpu.make_async_copy(queries, query_v, local_sem.at[3]),
        pltpu.make_async_copy(
            w_out.at[:, pl.ds(0, width)], out_w.at[2 * seq], local_sem.at[4]
        ),
        pltpu.make_async_copy(
            w_out.at[:, pl.ds(width, width)], out_w.at[2 * seq + 1], local_sem.at[5]
        ),
    ]
    hidden_load = pltpu.make_async_copy(hidden, query_v, local_sem.at[6])
    for load in loads:
        load.start()

    barrier = pltpu.get_barrier_semaphore()
    for ids in (pair_id, cross_id, seq_id):
        pl.semaphore_signal(barrier, inc=1, device_id=device(ids), device_id_type=MESH)

    @pl.when(mp > 0)
    def _():
        pl.semaphore_signal(barrier, inc=1, device_id=device({"mp": mp - 1}), device_id_type=MESH)

    @pl.when(mp < 3)
    def _():
        pl.semaphore_signal(barrier, inc=1, device_id=device({"mp": mp + 1}), device_id_type=MESH)

    neighbours = 5 - (mp == 0).astype(jnp.int32) - (mp == 3).astype(jnp.int32)
    pl.semaphore_wait(barrier, neighbours)

    def part_of(owner, size):
        return pl.ds(pl.multiple_of(owner * size, size), size)

    half_rows = part_of(core, 2 * quarter)
    near_rows = part_of(2 * core + chip, quarter)
    far_rows = part_of(2 * core + 1 - chip, quarter)
    rows_of_step = (half_rows, near_rows)

    def w_copy(step):
        local_block = seq if step == 0 else 1 - seq
        block = 2 * seq + local_block
        return pltpu.make_async_remote_copy(
            src_ref=w_out.at[rows_of_step[step], pl.ds(pl.multiple_of(local_block * width, width), width)],
            dst_ref=out_w.at[block, rows_of_step[step]],
            send_sem=w_ssem.at[step],
            recv_sem=w_rsem.at[step],
            device_id=device(seq_id),
            device_id_type=MESH,
        )

    is_end = (mp == 0) | (mp == 3)
    first = jnp.where(mp < 2, 3, 0)
    third = 1 + seq
    late = 2 - seq
    inward = jnp.where(mp < 2, 1, 2)
    owns_first = (first // 2) == seq

    def end_w_direct(step):
        local_block = seq if step == 0 else 1 - seq
        return pltpu.make_async_remote_copy(
            src_ref=w_out.at[near_rows, pl.ds(pl.multiple_of(local_block * width, width), width)],
            dst_ref=end_w.at[step, near_rows],
            send_sem=ew_ssem.at[step], recv_sem=ew_rsem.at[step],
            device_id=device({"mp": inward}), device_id_type=MESH,
        )

    def end_w_received():
        return pltpu.make_async_remote_copy(
            src_ref=out_w.at[first, near_rows],
            dst_ref=end_w.at[0, near_rows],
            send_sem=ew_ssem.at[0], recv_sem=ew_rsem.at[0],
            device_id=device({"mp": inward}), device_id_type=MESH,
        )

    other = 1 - seq
    blocks = (
        out_w.at[2 * other + other],
        out_w.at[2 * other + 1 - other],
        end_w.at[0],
        end_w.at[1],
    )

    def cross_spread(b):
        return pltpu.make_async_remote_copy(
            src_ref=blocks[b].at[near_rows], dst_ref=blocks[b].at[near_rows],
            send_sem=wx_ssem.at[b], recv_sem=wx_rsem.at[b],
            device_id=device(cross_id), device_id_type=MESH,
        )

    def pair_spread(b, i):
        part = far_rows if i else (near_rows if b else half_rows)
        return pltpu.make_async_remote_copy(
            src_ref=blocks[b].at[part], dst_ref=blocks[b].at[part],
            send_sem=wp_ssem.at[b, i], recv_sem=wp_rsem.at[b, i],
            device_id=device(pair_id), device_id_type=MESH,
        )

    def spread_start(b):
        if b:
            cross_spread(b).start()
        pair_spread(b, 0).start()

    def spread_far(b):
        cross_spread(b).wait_recv()
        pair_spread(b, 1).start()

    def spread_end(b):
        pair_spread(b, 0).wait_recv()
        if b:
            pair_spread(b, 1).wait_recv()

    def spread_sent(b):
        pair_spread(b, 0).wait_send()
        if b:
            cross_spread(b).wait_send()
            pair_spread(b, 1).wait_send()

    inner = jnp.logical_not(is_end)
    spreads_first = jnp.logical_not(is_end & jnp.logical_not(owns_first))

    def end_copy(j):
        return pltpu.make_async_remote_copy(
            src_ref=attended.at[j], dst_ref=end_rows.at[j],
            send_sem=end_ssem.at[j], recv_sem=end_rsem.at[j],
            device_id=device({"mp": inward}), device_id_type=MESH,
        )

    @pl.when(owns_first)
    def _():
        w_copy(0).start()

    @pl.when(is_end)
    def _():
        @pl.when(owns_first)
        def _():
            end_w_direct(0).start()

        end_w_direct(1).start()

    loads[0].wait()

    @pl.loop(0, caption_count)
    def _(c):
        values = cap_raw[c].astype(F32)
        scaled[c] = (values * gain[...]).astype(BF16)
        square = values * values
        folded = square[:, :HEAD]
        for group in range(1, features // HEAD):
            folded = folded + square[:, group * HEAD : (group + 1) * HEAD]
        squares[c] = folded.astype(BF16)

    loads[1].wait()
    loads[2].wait()
    tile = 256

    def slot_partial(u, out_core, dst):
        ids = [image_caption[4 * (2 * x + out_core) + u // 2] % caption_count for x in range(2)]
        lhs = jnp.concatenate([scaled[i] for i in ids], axis=0)
        half_index = u % 2

        @pl.loop(0, width // tile)
        def _(t):
            cols = pl.ds(pl.multiple_of(t * tile, tile), tile)
            part = jnp.dot(lhs, kv_w[half_index, :, cols], preferred_element_type=F32).astype(BF16)
            for x in range(2):
                dst[u, x, :, cols] = part[x * slots : (x + 1) * slots]

        for x in range(2):
            dst[u, x, :, width:] = squares[ids[x]]

    def pair_copy(j):
        return pltpu.make_async_remote_copy(
            src_ref=pair_send.at[j], dst_ref=pair_recv.at[j],
            send_sem=pair_ssem.at[j], recv_sem=pair_rsem.at[j],
            device_id=device(pair_id), device_id_type=MESH,
        )

    def cross_copy(j):
        return pltpu.make_async_remote_copy(
            src_ref=own.at[j, 1 - chip], dst_ref=cross_recv.at[j],
            send_sem=cross_ssem.at[j], recv_sem=cross_rsem.at[j],
            device_id=device(cross_id), device_id_type=MESH,
        )

    def row_copy(j):
        return pltpu.make_async_remote_copy(
            src_ref=rows.at[j, seq], dst_ref=rows.at[j, seq],
            send_sem=row_ssem.at[j], recv_sem=row_rsem.at[j],
            device_id=device(seq_id), device_id_type=MESH,
        )

    def stage_partial(j):
        slot_partial(j, 1 - core, pair_send)
        pair_copy(j).start()
        slot_partial(j, core, own)

    def stage_pair(j):
        pair_copy(j).wait_recv()
        far = 1 - chip
        own[j, far] = (own[j, far].astype(F32) + pair_recv[j, far].astype(F32)).astype(BF16)
        cross_copy(j).start()

    def stage_rows(j):
        cross_copy(j).wait_recv()
        tail = pl.ds(width, HEAD)
        mean = jnp.sum(
            own[j, chip, :, tail].astype(F32)
            + pair_recv[j, chip, :, tail].astype(F32)
            + cross_recv[j, :, tail].astype(F32),
            axis=1, keepdims=True,
        ) / total_features
        inverse = lax.rsqrt(mean + 1e-06)

        @pl.loop(0, width // tile)
        def _(t):
            cols = pl.ds(pl.multiple_of(t * tile, tile), tile)
            value = (
                own[j, chip, :, cols].astype(F32)
                + pair_recv[j, chip, :, cols].astype(F32)
                + cross_recv[j, :, cols].astype(F32)
            )
            rows[j, seq, :, cols] = (value * inverse).astype(BF16)

        row_copy(j).start()

    def stage_attend(j):
        row_copy(2 * j).wait_recv()
        row_copy(2 * j + 1).wait_recv()
        caption = image_caption[4 * seg + j]
        from_first = caption < caption_count
        live = caption_lengths[caption]
        mask = lax.broadcasted_iota(jnp.int32, (patches, slots), 1) < live

        def picked(u, cols):
            return jnp.where(from_first, rows[u, 0, :, cols], rows[u, 1, :, cols])

        for h in range(head_count):
            cols = slice(h * HEAD, (h + 1) * HEAD)
            scores = lax.dot_general(
                query_v[j, :, cols], picked(2 * j, cols),
                (((1,), (1,)), ((), ())), preferred_element_type=F32,
            ) * HEAD ** (-0.5)
            scores = jnp.where(mask, scores, -1e30)
            top = jnp.max(scores, axis=1, keepdims=True)
            expd = jnp.exp(scores - top)
            weights = (expd / jnp.sum(expd, axis=1, keepdims=True)).astype(BF16)
            attended[j, :, cols] = jnp.dot(
                weights, picked(2 * j + 1, cols), preferred_element_type=F32
            ).astype(BF16)

    def up_copy(n, j):
        return pltpu.make_async_remote_copy(
            src_ref=moving.at[n, j], dst_ref=moving.at[n, j],
            send_sem=z_ssem.at[n, j], recv_sem=z_rsem.at[n, j],
            device_id=device({"mp": lax.min(mp + 1, 3)}), device_id_type=MESH,
        )

    def down_copy(n, j):
        return pltpu.make_async_remote_copy(
            src_ref=moving.at[n, j], dst_ref=moving.at[n, j],
            send_sem=z_ssem.at[n, j], recv_sem=z_rsem.at[n, j],
            device_id=device({"mp": lax.max(mp - 1, 0)}), device_id_type=MESH,
        )

    def last_copy(n, j):
        return pltpu.make_async_remote_copy(
            src_ref=moving.at[n, j], dst_ref=from_right.at[j],
            send_sem=z_ssem.at[n, j], recv_sem=left_rsem.at[j],
            device_id=device({"mp": lax.max(mp - 1, 0)}), device_id_type=MESH,
        )

    def send_on(n, j):
        @pl.when(n > mp)
        def _():
            up_copy(n, j).start()

        @pl.when(n < mp - 1)
        def _():
            down_copy(n, j).start()

        @pl.when(n == mp - 1)
        def _():
            last_copy(n, j).start()

    def source_step(n, j):
        @pl.loop(0, width // tile)
        def _(t):
            cols = pl.ds(pl.multiple_of(t * tile, tile), tile)
            moving[n, j, :, cols] = jnp.dot(
                attended[j], out_w[n, :, cols], preferred_element_type=F32
            ).astype(BF16)

        send_on(n, j)

    def relay_step(n, j):
        up_copy(n, j).wait_recv()

        @pl.loop(0, width // tile)
        def _(t):
            cols = pl.ds(pl.multiple_of(t * tile, tile), tile)
            share = jnp.dot(attended[j], out_w[n, :, cols], preferred_element_type=F32)
            moving[n, j, :, cols] = (share + moving[n, j, :, cols].astype(F32)).astype(BF16)

        send_on(n, j)

    def joint_step(n, step, j):
        @pl.loop(0, width // tile)
        def _(t):
            cols = pl.ds(pl.multiple_of(t * tile, tile), tile)
            share = jnp.dot(attended[j], out_w[n, :, cols], preferred_element_type=F32)
            share = share + jnp.dot(end_rows[j], end_w[step, :, cols], preferred_element_type=F32)
            moving[n, j, :, cols] = share.astype(BF16)

        send_on(n, j)

    from_below = (mp > 0) & jnp.logical_not((mp == 1) & (third == 1))
    from_above = (mp < 3) & jnp.logical_not((mp == 2) & (third == 2))
    has_end_term = jnp.logical_not(is_end) & (third == mp)

    def final_step(j):
        @pl.when(from_below)
        def _():
            up_copy(mp, j).wait_recv()

        @pl.when(from_above)
        def _():
            last_copy(mp, j).wait_recv()

        def finish(t, terms):
            cols = pl.ds(pl.multiple_of(t * tile, tile), tile)
            share = jnp.dot(attended[j], out_w[mp, :, cols], preferred_element_type=F32)
            for term in terms:
                share = share + term(cols)
            result[j, :, cols] = (
                query_v[j, :, cols].astype(F32) + gate[pl.ds(j, 1), cols] * share
            ).astype(BF16)

        def below(cols):
            return moving[mp, j, :, cols].astype(F32)

        def above(cols):
            return from_right[j, :, cols].astype(F32)

        def end_term(cols):
            return jnp.dot(end_rows[j], end_w[1, :, cols], preferred_element_type=F32)

        for condition, terms in (
            (mp == 0, (above,)),
            (mp == 3, (below,)),
            (has_end_term & (mp == 1), (above, end_term)),
            (has_end_term & (mp == 2), (below, end_term)),
            (jnp.logical_not(is_end) & (third != mp), (below, above)),
        ):
            @pl.when(condition)
            def _():
                pl.loop(0, width // tile)(lambda t: finish(t, terms))

    def wait_send(n, j):
        up_copy(n, j).wait_send()

    near = inner & owns_first
    distant = inner & jnp.logical_not(owns_first)

    @pl.loop(0, rounds + 4)
    def _(u):
        @pl.when((u >= 1) & (u < rounds + 1))
        def _():
            stage_pair(u - 1)

        @pl.when(u < 2)
        def _():
            stage_partial(u)

        @pl.when((u >= 2) & (u < rounds + 2))
        def _():
            stage_rows(u - 2)

        @pl.when((u == 3) & jnp.logical_not(owns_first))
        def _():
            w_copy(0).start()

            @pl.when(is_end)
            def _():
                w_copy(0).wait_recv()
                end_w_received().start()

        @pl.when((u == 3) & near)
        def _():
            end_w_direct(0).wait_recv()
            spread_start(2)

        @pl.when((u >= 4) & (u % 2 == 0))
        def _():
            j = (u - 4) // 2

            @pl.when(j == 0)
            def _():
                loads[3].wait()

            stage_attend(j)

            @pl.when(is_end)
            def _():
                end_copy(j).start()

        @pl.when((u == 4) & near)
        def _():
            spread_far(2)
            end_w_direct(1).wait_recv()
            spread_start(3)

        @pl.when((u == 4) & distant)
        def _():
            w_copy(0).wait_recv()
            spread_start(0)
            end_w_direct(0).wait_recv()
            spread_start(2)

        @pl.when((u >= 2) & (u < rounds))
        def _():
            stage_partial(u)

        @pl.when(u == 5)
        def _():
            loads[4].wait()
            loads[5].wait()

            @pl.when(distant)
            def _():
                spread_far(2)
                spread_end(0)

            @pl.when(inner)
            def _():
                spread_end(2)

        @pl.when(u == 6)
        def _():
            w_copy(1).start()

        @pl.when((u == 7) & distant)
        def _():
            end_w_direct(1).wait_recv()
            spread_start(3)

        @pl.when((u == 9) & distant)
        def _():
            spread_far(3)

        @pl.when((u >= 5) & (u % 2 == 1) & inner)
        def _():
            j = (u - 5) // 2
            end_copy(j).wait_recv()
            joint_step(first, 0, j)

            @pl.when((j == 0) & near)
            def _():
                spread_far(3)
                spread_end(3)

            @pl.when(near)
            def _():
                joint_step(third, 1, j)

        @pl.when((u == 7) & owns_first)
        def _():
            w_copy(0).wait_recv()
            spread_start(0)
            spread_end(0)

        @pl.when((u == 7) | (u == 9))
        def _():
            @pl.when(inner)
            def _():
                relay_step(3 - first, (u - 7) // 2)

        @pl.when(u == 9)
        def _():
            w_copy(1).wait_recv()
            spread_start(1)

        @pl.when(u == 11)
        def _():
            spread_far(1)

    hidden_load.start()

    spread_end(1)

    @pl.when(distant)
    def _():
        spread_end(3)

    @pl.when(is_end)
    def _():
        @pl.loop(0, images)
        def _(j):
            @pl.when(j >= 2)
            def _():
                wait_send(late, j - 2)

            source_step(late, j)

    @pl.when(inner)
    def _():
        @pl.loop(0, images + 2)
        def _(t):
            half_count = images // 2
            outward = (t == half_count) | (t == images + 1)
            late_j = t - (t > half_count).astype(jnp.int32)

            @pl.when(outward)
            def _():
                relay_step(3 - first, images - 2 + (t > half_count).astype(jnp.int32))

            @pl.when(jnp.logical_not(outward) & (late != mp))
            def _():
                relay_step(late, late_j)

    hidden_load.wait()

    @pl.loop(0, images)
    def _(j):
        final_step(j)

    for step in range(2):
        w_copy(step).wait_send()

    spread_sent(1)

    @pl.when(spreads_first)
    def _():
        spread_sent(0)

    @pl.loop(0, rounds)
    def _(u):
        pair_copy(u).wait_send()
        cross_copy(u).wait_send()
        row_copy(u).wait_send()

    @pl.when(is_end)
    def _():
        for step in range(2):
            end_w_direct(step).wait_send()

        for j in range(images):
            end_copy(j).wait_send()

        wait_send(late, images - 2)
        wait_send(late, images - 1)

    @pl.when(jnp.logical_not(is_end))
    def _():
        for step in range(2):
            spread_sent(2 + step)

        @pl.loop(0, images)
        def _(j):
            wait_send(first, j)
            wait_send(3 - first, j)

            @pl.when(third != mp)
            def _():
                wait_send(third, j)

            @pl.when(late != mp)
            def _():
                wait_send(late, j)


def fused_shards(
    captions,
    caption_lengths,
    image_caption,
    t5_gain,
    w_key,
    w_value,
    queries,
    hidden,
    out_gate,
    w_out,
):
    caption_count, slots, features = captions.shape
    images, patches, width = queries.shape
    packed = width + HEAD
    rounds = 2 * images
    smem = pl.BlockSpec(memory_space=pltpu.SMEM)
    vmem = pl.BlockSpec(memory_space=pltpu.VMEM)
    hbm = pl.BlockSpec(memory_space=pl.ANY)
    dma = pltpu.SemaphoreType.DMA
    return pl.pallas_call(
        fused_kernel,
        out_shape=jax.ShapeDtypeStruct(queries.shape, BF16),
        in_specs=[smem, smem, vmem, vmem, hbm, hbm, hbm, hbm, hbm, hbm],
        out_specs=vmem,
        scratch_shapes=[
            pltpu.VMEM(captions.shape, BF16),
            pltpu.VMEM((2,) + w_key.shape, BF16),
            pltpu.VMEM(queries.shape, BF16),
            pltpu.VMEM((4, w_out.shape[0], width), BF16),
            pltpu.VMEM(captions.shape, BF16),
            pltpu.VMEM((caption_count, slots, HEAD), BF16),
            pltpu.VMEM((rounds, 2, slots, packed), BF16),
            pltpu.VMEM((rounds, 2, slots, packed), BF16),
            pltpu.VMEM((rounds, 2, slots, packed), BF16),
            pltpu.VMEM((rounds, slots, packed), BF16),
            pltpu.VMEM((rounds, 2, slots, width), BF16),
            pltpu.VMEM(queries.shape, BF16),
            pltpu.VMEM((4,) + queries.shape, BF16),
            pltpu.VMEM(queries.shape, BF16),
            pltpu.VMEM(queries.shape, BF16),
            pltpu.VMEM((2, w_out.shape[0], width), BF16),
            dma((7,)),
            dma((rounds,)), dma((rounds,)),
            dma((rounds,)), dma((rounds,)),
            dma((rounds,)), dma((rounds,)),
            dma((2,)), dma((2,)),
            dma((4, images)), dma((4, images)), dma((images,)),
            dma((images,)), dma((images,)),
            dma((2,)), dma((2,)),
            dma((4,)), dma((4,)), dma((4, 2)), dma((4, 2)),
        ],
        compiler_params=pltpu.CompilerParams(
            collective_id=0, has_side_effects=True, vmem_limit_bytes=60 * 1024 * 1024
        ),
        cost_estimate=pl.CostEstimate(
            flops=20_000_000_000, bytes_accessed=20_000_000, transcendentals=1_100_000
        ),
    )(
        image_caption, caption_lengths, t5_gain.reshape(1, -1), out_gate,
        captions, w_key, w_value, queries, hidden, w_out,
    )


def solution(mesh):
    in_specs = (
        P("seq", None, "segment"),
        P(),
        P(),
        P("segment"),
        P("segment", "mp"),
        P("segment", "mp"),
        P("segment", "seq", "mp"),
        P("segment", "seq", "mp"),
        P("segment", "mp"),
        P("mp", "seq"),
    )
    out_specs = P("segment", "seq", "mp")
    fused = (mesh.shape["segment"], mesh.shape["seq"], mesh.shape["mp"]) == (4, 2, 4)
    shards = fused_shards if fused else general_shards
    return jax.shard_map(shards, mesh=mesh, in_specs=in_specs, out_specs=out_specs, check_vma=False)
```

```python
import functools

import jax
import jax.numpy as jnp
from jax import lax
from jax.experimental import pallas as pl
from jax.experimental.pallas import tpu as pltpu
from jax.sharding import PartitionSpec as P

HEAD = 128
MESH = pl.DeviceIdType.MESH
BF16 = jnp.bfloat16
F32 = jnp.float32


def general_shards(
    captions,
    caption_lengths,
    image_caption,
    t5_gain,
    w_key,
    w_value,
    queries,
    hidden,
    out_gate,
    w_out,
):
    caption_count, caption_slots, feature_share = captions.shape
    image_count, patch_count, head_cols = queries.shape
    segment_count = lax.axis_size("segment")
    caption_values = captions.astype(jnp.float32)
    squares_total = lax.psum(jnp.sum(caption_values * caption_values, axis=2), "segment")
    inverse_rms = lax.rsqrt(squares_total / (feature_share * segment_count) + 1e-06)
    normed = (caption_values * inverse_rms[:, :, None] * t5_gain).astype(jnp.bfloat16)
    flattened = normed.reshape(caption_count * caption_slots, feature_share)
    key_partial = jnp.dot(flattened, w_key, preferred_element_type=jnp.float32)
    value_partial = jnp.dot(flattened, w_value, preferred_element_type=jnp.float32)
    first_image = lax.axis_index("segment") * image_count
    owner_ids = lax.dynamic_slice_in_dim(image_caption, first_image, image_count)
    stacked = jnp.concatenate([key_partial, value_partial], axis=1)
    column_share = lax.psum_scatter(
        stacked.astype(jnp.bfloat16), "segment", scatter_dimension=1, tiled=True
    ).astype(jnp.float32)
    piece_width = column_share.shape[1]
    column_share = column_share.astype(jnp.bfloat16).reshape(
        1, caption_count, caption_slots, piece_width
    )
    pieces = lax.all_gather(column_share, ("segment", "seq"), axis=0, tiled=True)
    pieces = pieces.reshape(segment_count, -1, caption_slots, piece_width)
    encoded = pieces.transpose(1, 2, 0, 3).reshape(
        pieces.shape[1], caption_slots, segment_count * piece_width
    )
    chosen = jnp.take(encoded, owner_ids, axis=0)
    live_lengths = jnp.take(caption_lengths, owner_ids)
    live_mask = jnp.arange(caption_slots, dtype=jnp.int32)[None, :] < live_lengths[:, None]
    head_count = head_cols // HEAD
    query_heads = queries.reshape(image_count, patch_count, head_count, HEAD)
    key_heads = chosen[:, :, :head_cols].reshape(image_count, caption_slots, head_count, HEAD)
    value_heads = chosen[:, :, head_cols:].reshape(image_count, caption_slots, head_count, HEAD)
    scores = jnp.einsum(
        "iphd,ikhd->ihpk", query_heads, key_heads, preferred_element_type=jnp.float32
    ) * HEAD ** (-0.5)
    scores = jnp.where(live_mask[:, None, None, :], scores, -1e30)
    weights = jax.nn.softmax(scores, axis=3).astype(jnp.bfloat16)
    attended = jnp.einsum(
        "ihpk,ikhd->iphd", weights, value_heads, preferred_element_type=jnp.float32
    )
    attended = attended.astype(jnp.bfloat16).reshape(image_count * patch_count, head_cols)
    partial_value = jnp.dot(
        attended,
        lax.all_gather(w_out, "seq", axis=1, tiled=True),
        preferred_element_type=jnp.float32,
    )
    mixed_heads = lax.psum_scatter(
        partial_value.astype(jnp.bfloat16), "mp", scatter_dimension=1, tiled=True
    ).astype(jnp.float32)
    result_rows = hidden.astype(jnp.float32) + out_gate[:, None, :] * mixed_heads.reshape(
        image_count, patch_count, head_cols
    )
    return result_rows.astype(jnp.bfloat16)


def fused_kernel(
    image_caption, caption_lengths, gain, gate, captions, w_key, w_value, queries, hidden, w_out,
    result,
    cap_raw, kv_w, query_v, out_w, scaled, squares,
    pair_send, pair_recv, own, cross_recv, rows, attended, moving, from_right, end_rows, end_w,
    local_sem, pair_ssem, pair_rsem, cross_ssem, cross_rsem, row_ssem, row_rsem,
    w_ssem, w_rsem, z_ssem, z_rsem, left_rsem,
    end_ssem, end_rsem, ew_ssem, ew_rsem, wx_ssem, wx_rsem, wp_ssem, wp_rsem,
):
    seg = lax.axis_index("segment")
    seq = lax.axis_index("seq")
    mp = lax.axis_index("mp")
    chip, core = seg // 2, seg % 2
    pair_id = {"segment": seg + 1 - 2 * core}
    cross_id = {"segment": (seg + 2) % 4}
    seq_id = {"seq": 1 - seq}
    caption_count, slots, features = cap_raw.shape
    images, patches, width = query_v.shape
    rounds = 2 * images
    head_count = width // HEAD
    quarter = out_w.shape[1] // 4
    total_features = 4 * features

    def device(ids):
        return {"segment": seg, "seq": seq, "mp": mp, **ids}

    loads = [
        pltpu.make_async_copy(captions, cap_raw, local_sem.at[0]),
        pltpu.make_async_copy(w_key, kv_w.at[0], local_sem.at[1]),
        pltpu.make_async_copy(w_value, kv_w.at[1], local_sem.at[2]),
        pltpu.make_async_copy(queries, query_v, local_sem.at[3]),
        pltpu.make_async_copy(
            w_out.at[:, pl.ds(0, width)], out_w.at[2 * seq], local_sem.at[4]
        ),
        pltpu.make_async_copy(
            w_out.at[:, pl.ds(width, width)], out_w.at[2 * seq + 1], local_sem.at[5]
        ),
    ]
    hidden_load = pltpu.make_async_copy(hidden, query_v, local_sem.at[6])
    for load in loads:
        load.start()

    barrier = pltpu.get_barrier_semaphore()
    for ids in (pair_id, cross_id, seq_id):
        pl.semaphore_signal(barrier, inc=1, device_id=device(ids), device_id_type=MESH)

    @pl.when(mp > 0)
    def _():
        pl.semaphore_signal(barrier, inc=1, device_id=device({"mp": mp - 1}), device_id_type=MESH)

    @pl.when(mp < 3)
    def _():
        pl.semaphore_signal(barrier, inc=1, device_id=device({"mp": mp + 1}), device_id_type=MESH)

    neighbours = 5 - (mp == 0).astype(jnp.int32) - (mp == 3).astype(jnp.int32)
    pl.semaphore_wait(barrier, neighbours)

    def part_of(owner, size):
        return pl.ds(pl.multiple_of(owner * size, size), size)

    half_rows = part_of(core, 2 * quarter)
    near_rows = part_of(seg, quarter)
    far_rows = part_of((seg + 2) % 4, quarter)
    rows_of_step = (half_rows, near_rows)

    def w_copy(step):
        local_block = seq if step == 0 else 1 - seq
        block = 2 * seq + local_block
        return pltpu.make_async_remote_copy(
            src_ref=w_out.at[rows_of_step[step], pl.ds(pl.multiple_of(local_block * width, width), width)],
            dst_ref=out_w.at[block, rows_of_step[step]],
            send_sem=w_ssem.at[step],
            recv_sem=w_rsem.at[step],
            device_id=device(seq_id),
            device_id_type=MESH,
        )

    is_end = (mp == 0) | (mp == 3)
    first = jnp.where(mp < 2, 3, 0)
    third = 1 + seq
    late = 2 - seq
    inward = jnp.where(mp < 2, 1, 2)
    owns_first = (first // 2) == seq

    def end_w_direct(step):
        local_block = seq if step == 0 else 1 - seq
        return pltpu.make_async_remote_copy(
            src_ref=w_out.at[rows_of_step[step], pl.ds(pl.multiple_of(local_block * width, width), width)],
            dst_ref=end_w.at[step, rows_of_step[step]],
            send_sem=ew_ssem.at[step], recv_sem=ew_rsem.at[step],
            device_id=device({"mp": inward}), device_id_type=MESH,
        )

    def end_w_received():
        return pltpu.make_async_remote_copy(
            src_ref=out_w.at[first, half_rows],
            dst_ref=end_w.at[0, half_rows],
            send_sem=ew_ssem.at[0], recv_sem=ew_rsem.at[0],
            device_id=device({"mp": inward}), device_id_type=MESH,
        )

    other = 1 - seq
    blocks = (
        out_w.at[2 * other + other],
        out_w.at[2 * other + 1 - other],
        end_w.at[0],
        end_w.at[1],
    )

    def cross_spread(b):
        return pltpu.make_async_remote_copy(
            src_ref=blocks[b].at[near_rows], dst_ref=blocks[b].at[near_rows],
            send_sem=wx_ssem.at[b], recv_sem=wx_rsem.at[b],
            device_id=device(cross_id), device_id_type=MESH,
        )

    def pair_spread(b, i):
        part = far_rows if i else (near_rows if b % 2 else half_rows)
        return pltpu.make_async_remote_copy(
            src_ref=blocks[b].at[part], dst_ref=blocks[b].at[part],
            send_sem=wp_ssem.at[b, i], recv_sem=wp_rsem.at[b, i],
            device_id=device(pair_id), device_id_type=MESH,
        )

    def spread_start(b):
        if b % 2:
            cross_spread(b).start()
        pair_spread(b, 0).start()

    def spread_far(b):
        cross_spread(b).wait_recv()
        pair_spread(b, 1).start()

    def spread_end(b):
        pair_spread(b, 0).wait_recv()
        if b % 2:
            pair_spread(b, 1).wait_recv()

    def spread_sent(b):
        pair_spread(b, 0).wait_send()
        if b % 2:
            cross_spread(b).wait_send()
            pair_spread(b, 1).wait_send()

    inner = jnp.logical_not(is_end)
    spreads_first = jnp.logical_not(is_end & jnp.logical_not(owns_first))

    def end_copy(j):
        return pltpu.make_async_remote_copy(
            src_ref=attended.at[j], dst_ref=end_rows.at[j],
            send_sem=end_ssem.at[j], recv_sem=end_rsem.at[j],
            device_id=device({"mp": inward}), device_id_type=MESH,
        )

    w_copy(0).start()

    @pl.when(is_end)
    def _():
        @pl.when(owns_first)
        def _():
            end_w_direct(0).start()

        end_w_direct(1).start()

    loads[0].wait()

    @pl.loop(0, caption_count)
    def _(c):
        values = cap_raw[c].astype(F32)
        scaled[c] = (values * gain[...]).astype(BF16)
        square = values * values
        folded = square[:, :HEAD]
        for group in range(1, features // HEAD):
            folded = folded + square[:, group * HEAD : (group + 1) * HEAD]
        squares[c] = folded.astype(BF16)

    loads[1].wait()
    loads[2].wait()
    tile = 256

    def slot_partial(u, out_core, dst):
        ids = [image_caption[4 * (2 * x + out_core) + u // 2] % caption_count for x in range(2)]
        lhs = jnp.concatenate([scaled[i] for i in ids], axis=0)
        half_index = u % 2

        @pl.loop(0, width // tile)
        def _(t):
            cols = pl.ds(pl.multiple_of(t * tile, tile), tile)
            part = jnp.dot(lhs, kv_w[half_index, :, cols], preferred_element_type=F32).astype(BF16)
            for x in range(2):
                dst[u, x, :, cols] = part[x * slots : (x + 1) * slots]

        for x in range(2):
            dst[u, x, :, width:] = squares[ids[x]]

    def pair_copy(j):
        return pltpu.make_async_remote_copy(
            src_ref=pair_send.at[j], dst_ref=pair_recv.at[j],
            send_sem=pair_ssem.at[j], recv_sem=pair_rsem.at[j],
            device_id=device(pair_id), device_id_type=MESH,
        )

    def cross_copy(j):
        return pltpu.make_async_remote_copy(
            src_ref=own.at[j, 1 - chip], dst_ref=cross_recv.at[j],
            send_sem=cross_ssem.at[j], recv_sem=cross_rsem.at[j],
            device_id=device(cross_id), device_id_type=MESH,
        )

    def row_copy(j):
        return pltpu.make_async_remote_copy(
            src_ref=rows.at[j, seq], dst_ref=rows.at[j, seq],
            send_sem=row_ssem.at[j], recv_sem=row_rsem.at[j],
            device_id=device(seq_id), device_id_type=MESH,
        )

    def stage_partial(j):
        slot_partial(j, 1 - core, pair_send)
        pair_copy(j).start()
        slot_partial(j, core, own)

    def stage_pair(j):
        pair_copy(j).wait_recv()
        far = 1 - chip
        own[j, far] = (own[j, far].astype(F32) + pair_recv[j, far].astype(F32)).astype(BF16)
        cross_copy(j).start()

    def stage_rows(j):
        cross_copy(j).wait_recv()
        tail = pl.ds(width, HEAD)
        mean = jnp.sum(
            own[j, chip, :, tail].astype(F32)
            + pair_recv[j, chip, :, tail].astype(F32)
            + cross_recv[j, :, tail].astype(F32),
            axis=1, keepdims=True,
        ) / total_features
        inverse = lax.rsqrt(mean + 1e-06)

        @pl.loop(0, width // tile)
        def _(t):
            cols = pl.ds(pl.multiple_of(t * tile, tile), tile)
            value = (
                own[j, chip, :, cols].astype(F32)
                + pair_recv[j, chip, :, cols].astype(F32)
                + cross_recv[j, :, cols].astype(F32)
            )
            rows[j, seq, :, cols] = (value * inverse).astype(BF16)

        row_copy(j).start()

    def stage_attend(j):
        row_copy(2 * j).wait_recv()
        row_copy(2 * j + 1).wait_recv()
        caption = image_caption[4 * seg + j]
        from_first = caption < caption_count
        live = caption_lengths[caption]
        mask = lax.broadcasted_iota(jnp.int32, (patches, slots), 1) < live

        def picked(u, cols):
            return jnp.where(from_first, rows[u, 0, :, cols], rows[u, 1, :, cols])

        for h in range(head_count):
            cols = slice(h * HEAD, (h + 1) * HEAD)
            scores = lax.dot_general(
                query_v[j, :, cols], picked(2 * j, cols),
                (((1,), (1,)), ((), ())), preferred_element_type=F32,
            ) * HEAD ** (-0.5)
            scores = jnp.where(mask, scores, -1e30)
            top = jnp.max(scores, axis=1, keepdims=True)
            expd = jnp.exp(scores - top)
            weights = (expd / jnp.sum(expd, axis=1, keepdims=True)).astype(BF16)
            attended[j, :, cols] = jnp.dot(
                weights, picked(2 * j + 1, cols), preferred_element_type=F32
            ).astype(BF16)

    def up_copy(n, j):
        return pltpu.make_async_remote_copy(
            src_ref=moving.at[n, j], dst_ref=moving.at[n, j],
            send_sem=z_ssem.at[n, j], recv_sem=z_rsem.at[n, j],
            device_id=device({"mp": lax.min(mp + 1, 3)}), device_id_type=MESH,
        )

    def down_copy(n, j):
        return pltpu.make_async_remote_copy(
            src_ref=moving.at[n, j], dst_ref=moving.at[n, j],
            send_sem=z_ssem.at[n, j], recv_sem=z_rsem.at[n, j],
            device_id=device({"mp": lax.max(mp - 1, 0)}), device_id_type=MESH,
        )

    def last_copy(n, j):
        return pltpu.make_async_remote_copy(
            src_ref=moving.at[n, j], dst_ref=from_right.at[j],
            send_sem=z_ssem.at[n, j], recv_sem=left_rsem.at[j],
            device_id=device({"mp": lax.max(mp - 1, 0)}), device_id_type=MESH,
        )

    def send_on(n, j):
        @pl.when(n > mp)
        def _():
            up_copy(n, j).start()

        @pl.when(n < mp - 1)
        def _():
            down_copy(n, j).start()

        @pl.when(n == mp - 1)
        def _():
            last_copy(n, j).start()

    def source_step(n, j):
        @pl.loop(0, width // tile)
        def _(t):
            cols = pl.ds(pl.multiple_of(t * tile, tile), tile)
            moving[n, j, :, cols] = jnp.dot(
                attended[j], out_w[n, :, cols], preferred_element_type=F32
            ).astype(BF16)

        send_on(n, j)

    def relay_step(n, j):
        up_copy(n, j).wait_recv()

        @pl.loop(0, width // tile)
        def _(t):
            cols = pl.ds(pl.multiple_of(t * tile, tile), tile)
            share = jnp.dot(attended[j], out_w[n, :, cols], preferred_element_type=F32)
            moving[n, j, :, cols] = (share + moving[n, j, :, cols].astype(F32)).astype(BF16)

        send_on(n, j)

    def joint_step(n, step, j):
        @pl.loop(0, width // tile)
        def _(t):
            cols = pl.ds(pl.multiple_of(t * tile, tile), tile)
            share = jnp.dot(attended[j], out_w[n, :, cols], preferred_element_type=F32)
            share = share + jnp.dot(end_rows[j], end_w[step, :, cols], preferred_element_type=F32)
            moving[n, j, :, cols] = share.astype(BF16)

        send_on(n, j)

    from_below = (mp > 0) & jnp.logical_not((mp == 1) & (third == 1))
    from_above = (mp < 3) & jnp.logical_not((mp == 2) & (third == 2))
    has_end_term = jnp.logical_not(is_end) & (third == mp)

    def final_step(j):
        @pl.when(from_below)
        def _():
            up_copy(mp, j).wait_recv()

        @pl.when(from_above)
        def _():
            last_copy(mp, j).wait_recv()

        def finish(t, terms):
            cols = pl.ds(pl.multiple_of(t * tile, tile), tile)
            share = jnp.dot(attended[j], out_w[mp, :, cols], preferred_element_type=F32)
            for term in terms:
                share = share + term(cols)
            result[j, :, cols] = (
                query_v[j, :, cols].astype(F32) + gate[pl.ds(j, 1), cols] * share
            ).astype(BF16)

        def below(cols):
            return moving[mp, j, :, cols].astype(F32)

        def above(cols):
            return from_right[j, :, cols].astype(F32)

        def end_term(cols):
            return jnp.dot(end_rows[j], end_w[1, :, cols], preferred_element_type=F32)

        for condition, terms in (
            (mp == 0, (above,)),
            (mp == 3, (below,)),
            (has_end_term & (mp == 1), (above, end_term)),
            (has_end_term & (mp == 2), (below, end_term)),
            (jnp.logical_not(is_end) & (third != mp), (below, above)),
        ):
            @pl.when(condition)
            def _():
                pl.loop(0, width // tile)(lambda t: finish(t, terms))

    def wait_send(n, j):
        up_copy(n, j).wait_send()

    near = inner & owns_first
    distant = inner & jnp.logical_not(owns_first)

    @pl.loop(0, rounds + 4)
    def _(u):
        @pl.when(u < rounds)
        def _():
            stage_partial(u)

        @pl.when((u >= 1) & (u < rounds + 1))
        def _():
            stage_pair(u - 1)

        @pl.when((u >= 2) & (u < rounds + 2))
        def _():
            stage_rows(u - 2)

        @pl.when((u == 3) & is_end & jnp.logical_not(owns_first))
        def _():
            w_copy(0).wait_recv()
            end_w_received().start()

        @pl.when((u >= 4) & (u % 2 == 0))
        def _():
            j = (u - 4) // 2

            @pl.when(j == 0)
            def _():
                loads[3].wait()

            stage_attend(j)

            @pl.when(is_end)
            def _():
                end_copy(j).start()

        @pl.when((u == 4) & near)
        def _():
            end_w_direct(0).wait_recv()
            spread_start(2)
            end_w_direct(1).wait_recv()
            spread_start(3)

        @pl.when((u == 4) & spreads_first)
        def _():
            w_copy(0).wait_recv()
            spread_start(0)

        @pl.when((u == 7) & distant)
        def _():
            end_w_direct(1).wait_recv()
            spread_start(3)

        @pl.when((u == 9) & distant)
        def _():
            spread_far(3)

        @pl.when(u == 8)
        def _():
            w_copy(1).wait_recv()
            spread_start(1)

        @pl.when(u == 10)
        def _():
            spread_far(1)

        @pl.when(u == 5)
        def _():
            w_copy(1).start()
            loads[4].wait()
            loads[5].wait()

            @pl.when(distant)
            def _():
                end_w_direct(0).wait_recv()
                spread_start(2)

            @pl.when(spreads_first)
            def _():
                spread_end(0)

            @pl.when(inner)
            def _():
                spread_end(2)

        @pl.when((u >= 5) & (u % 2 == 1) & inner)
        def _():
            j = (u - 5) // 2
            end_copy(j).wait_recv()
            joint_step(first, 0, j)

            @pl.when((j == 0) & near)
            def _():
                spread_far(3)
                spread_end(3)

            @pl.when(near)
            def _():
                joint_step(third, 1, j)

            @pl.when((j >= 1) & (j < images - 1))
            def _():
                relay_step(3 - first, j - 1)

    hidden_load.start()

    spread_end(1)

    @pl.when(distant)
    def _():
        spread_end(3)

    @pl.when(is_end)
    def _():
        @pl.loop(0, images)
        def _(j):
            @pl.when(j >= 2)
            def _():
                wait_send(late, j - 2)

            source_step(late, j)

    @pl.when(inner)
    def _():
        @pl.loop(0, images + 2)
        def _(t):
            half_count = images // 2
            outward = (t == half_count) | (t == images + 1)
            late_j = t - (t > half_count).astype(jnp.int32)

            @pl.when(outward)
            def _():
                relay_step(3 - first, images - 2 + (t > half_count).astype(jnp.int32))

            @pl.when(jnp.logical_not(outward) & (late != mp))
            def _():
                relay_step(late, late_j)

    hidden_load.wait()

    @pl.loop(0, images)
    def _(j):
        final_step(j)

    for step in range(2):
        w_copy(step).wait_send()

    spread_sent(1)

    @pl.when(spreads_first)
    def _():
        spread_sent(0)

    @pl.loop(0, rounds)
    def _(u):
        pair_copy(u).wait_send()
        cross_copy(u).wait_send()
        row_copy(u).wait_send()

    @pl.when(is_end)
    def _():
        for step in range(2):
            end_w_direct(step).wait_send()

        for j in range(images):
            end_copy(j).wait_send()

        wait_send(late, images - 2)
        wait_send(late, images - 1)

    @pl.when(jnp.logical_not(is_end))
    def _():
        for step in range(2):
            spread_sent(2 + step)

        @pl.loop(0, images)
        def _(j):
            wait_send(first, j)
            wait_send(3 - first, j)

            @pl.when(third != mp)
            def _():
                wait_send(third, j)

            @pl.when(late != mp)
            def _():
                wait_send(late, j)


def fused_shards(
    captions,
    caption_lengths,
    image_caption,
    t5_gain,
    w_key,
    w_value,
    queries,
    hidden,
    out_gate,
    w_out,
):
    caption_count, slots, features = captions.shape
    images, patches, width = queries.shape
    packed = width + HEAD
    rounds = 2 * images
    smem = pl.BlockSpec(memory_space=pltpu.SMEM)
    vmem = pl.BlockSpec(memory_space=pltpu.VMEM)
    hbm = pl.BlockSpec(memory_space=pl.ANY)
    dma = pltpu.SemaphoreType.DMA
    return pl.pallas_call(
        fused_kernel,
        out_shape=jax.ShapeDtypeStruct(queries.shape, BF16),
        in_specs=[smem, smem, vmem, vmem, hbm, hbm, hbm, hbm, hbm, hbm],
        out_specs=vmem,
        scratch_shapes=[
            pltpu.VMEM(captions.shape, BF16),
            pltpu.VMEM((2,) + w_key.shape, BF16),
            pltpu.VMEM(queries.shape, BF16),
            pltpu.VMEM((4, w_out.shape[0], width), BF16),
            pltpu.VMEM(captions.shape, BF16),
            pltpu.VMEM((caption_count, slots, HEAD), BF16),
            pltpu.VMEM((rounds, 2, slots, packed), BF16),
            pltpu.VMEM((rounds, 2, slots, packed), BF16),
            pltpu.VMEM((rounds, 2, slots, packed), BF16),
            pltpu.VMEM((rounds, slots, packed), BF16),
            pltpu.VMEM((rounds, 2, slots, width), BF16),
            pltpu.VMEM(queries.shape, BF16),
            pltpu.VMEM((4,) + queries.shape, BF16),
            pltpu.VMEM(queries.shape, BF16),
            pltpu.VMEM(queries.shape, BF16),
            pltpu.VMEM((2, w_out.shape[0], width), BF16),
            dma((7,)),
            dma((rounds,)), dma((rounds,)),
            dma((rounds,)), dma((rounds,)),
            dma((rounds,)), dma((rounds,)),
            dma((2,)), dma((2,)),
            dma((4, images)), dma((4, images)), dma((images,)),
            dma((images,)), dma((images,)),
            dma((2,)), dma((2,)),
            dma((4,)), dma((4,)), dma((4, 2)), dma((4, 2)),
        ],
        compiler_params=pltpu.CompilerParams(
            collective_id=0, has_side_effects=True, vmem_limit_bytes=60 * 1024 * 1024
        ),
        cost_estimate=pl.CostEstimate(
            flops=20_000_000_000, bytes_accessed=20_000_000, transcendentals=1_100_000
        ),
    )(
        image_caption, caption_lengths, t5_gain.reshape(1, -1), out_gate,
        captions, w_key, w_value, queries, hidden, w_out,
    )


def solution(mesh):
    in_specs = (
        P("seq", None, "segment"),
        P(),
        P(),
        P("segment"),
        P("segment", "mp"),
        P("segment", "mp"),
        P("segment", "seq", "mp"),
        P("segment", "seq", "mp"),
        P("segment", "mp"),
        P("mp", "seq"),
    )
    out_specs = P("segment", "seq", "mp")
    fused = (mesh.shape["segment"], mesh.shape["seq"], mesh.shape["mp"]) == (4, 2, 4)
    shards = fused_shards if fused else general_shards
    return jax.shard_map(shards, mesh=mesh, in_specs=in_specs, out_specs=out_specs, check_vma=False)
```

```python
import functools

import jax
import jax.numpy as jnp
from jax import lax
from jax.experimental import pallas as pl
from jax.experimental.pallas import tpu as pltpu
from jax.sharding import PartitionSpec as P

HEAD = 128
MESH = pl.DeviceIdType.MESH
BF16 = jnp.bfloat16
F32 = jnp.float32


def general_shards(
    captions,
    caption_lengths,
    image_caption,
    t5_gain,
    w_key,
    w_value,
    queries,
    hidden,
    out_gate,
    w_out,
):
    caption_count, caption_slots, feature_share = captions.shape
    image_count, patch_count, head_cols = queries.shape
    segment_count = lax.axis_size("segment")
    caption_values = captions.astype(jnp.float32)
    squares_total = lax.psum(jnp.sum(caption_values * caption_values, axis=2), "segment")
    inverse_rms = lax.rsqrt(squares_total / (feature_share * segment_count) + 1e-06)
    normed = (caption_values * inverse_rms[:, :, None] * t5_gain).astype(jnp.bfloat16)
    flattened = normed.reshape(caption_count * caption_slots, feature_share)
    key_partial = jnp.dot(flattened, w_key, preferred_element_type=jnp.float32)
    value_partial = jnp.dot(flattened, w_value, preferred_element_type=jnp.float32)
    first_image = lax.axis_index("segment") * image_count
    owner_ids = lax.dynamic_slice_in_dim(image_caption, first_image, image_count)
    stacked = jnp.concatenate([key_partial, value_partial], axis=1)
    column_share = lax.psum_scatter(
        stacked.astype(jnp.bfloat16), "segment", scatter_dimension=1, tiled=True
    ).astype(jnp.float32)
    piece_width = column_share.shape[1]
    column_share = column_share.astype(jnp.bfloat16).reshape(
        1, caption_count, caption_slots, piece_width
    )
    pieces = lax.all_gather(column_share, ("segment", "seq"), axis=0, tiled=True)
    pieces = pieces.reshape(segment_count, -1, caption_slots, piece_width)
    encoded = pieces.transpose(1, 2, 0, 3).reshape(
        pieces.shape[1], caption_slots, segment_count * piece_width
    )
    chosen = jnp.take(encoded, owner_ids, axis=0)
    live_lengths = jnp.take(caption_lengths, owner_ids)
    live_mask = jnp.arange(caption_slots, dtype=jnp.int32)[None, :] < live_lengths[:, None]
    head_count = head_cols // HEAD
    query_heads = queries.reshape(image_count, patch_count, head_count, HEAD)
    key_heads = chosen[:, :, :head_cols].reshape(image_count, caption_slots, head_count, HEAD)
    value_heads = chosen[:, :, head_cols:].reshape(image_count, caption_slots, head_count, HEAD)
    scores = jnp.einsum(
        "iphd,ikhd->ihpk", query_heads, key_heads, preferred_element_type=jnp.float32
    ) * HEAD ** (-0.5)
    scores = jnp.where(live_mask[:, None, None, :], scores, -1e30)
    weights = jax.nn.softmax(scores, axis=3).astype(jnp.bfloat16)
    attended = jnp.einsum(
        "ihpk,ikhd->iphd", weights, value_heads, preferred_element_type=jnp.float32
    )
    attended = attended.astype(jnp.bfloat16).reshape(image_count * patch_count, head_cols)
    partial_value = jnp.dot(
        attended,
        lax.all_gather(w_out, "seq", axis=1, tiled=True),
        preferred_element_type=jnp.float32,
    )
    mixed_heads = lax.psum_scatter(
        partial_value.astype(jnp.bfloat16), "mp", scatter_dimension=1, tiled=True
    ).astype(jnp.float32)
    result_rows = hidden.astype(jnp.float32) + out_gate[:, None, :] * mixed_heads.reshape(
        image_count, patch_count, head_cols
    )
    return result_rows.astype(jnp.bfloat16)


def fused_kernel(
    image_caption, caption_lengths, gain, gate, captions, w_key, w_value, queries, hidden, w_out,
    result,
    cap_raw, kv_w, query_v, out_w, scaled, squares,
    pair_send, pair_recv, own, cross_recv, rows, attended, moving, from_right, end_rows, end_w,
    local_sem, pair_ssem, pair_rsem, cross_ssem, cross_rsem, row_ssem, row_rsem,
    w_ssem, w_rsem, z_ssem, z_rsem, left_rsem,
    end_ssem, end_rsem, ew_ssem, ew_rsem, wx_ssem, wx_rsem, wp_ssem, wp_rsem,
):
    seg = lax.axis_index("segment")
    seq = lax.axis_index("seq")
    mp = lax.axis_index("mp")
    chip, core = seg // 2, seg % 2
    pair_id = {"segment": seg + 1 - 2 * core}
    cross_id = {"segment": (seg + 2) % 4}
    seq_id = {"seq": 1 - seq}
    caption_count, slots, features = cap_raw.shape
    images, patches, width = query_v.shape
    rounds = 2 * images
    head_count = width // HEAD
    quarter = out_w.shape[1] // 4
    total_features = 4 * features

    def device(ids):
        return {"segment": seg, "seq": seq, "mp": mp, **ids}

    loads = [
        pltpu.make_async_copy(captions, cap_raw, local_sem.at[0]),
        pltpu.make_async_copy(w_key, kv_w.at[0], local_sem.at[1]),
        pltpu.make_async_copy(w_value, kv_w.at[1], local_sem.at[2]),
        pltpu.make_async_copy(queries, query_v, local_sem.at[3]),
        pltpu.make_async_copy(
            w_out.at[:, pl.ds(0, width)], out_w.at[2 * seq], local_sem.at[4]
        ),
        pltpu.make_async_copy(
            w_out.at[:, pl.ds(width, width)], out_w.at[2 * seq + 1], local_sem.at[5]
        ),
    ]
    hidden_load = pltpu.make_async_copy(hidden, query_v, local_sem.at[6])
    for load in loads:
        load.start()

    barrier = pltpu.get_barrier_semaphore()
    for ids in (pair_id, cross_id, seq_id):
        pl.semaphore_signal(barrier, inc=1, device_id=device(ids), device_id_type=MESH)

    @pl.when(mp > 0)
    def _():
        pl.semaphore_signal(barrier, inc=1, device_id=device({"mp": mp - 1}), device_id_type=MESH)

    @pl.when(mp < 3)
    def _():
        pl.semaphore_signal(barrier, inc=1, device_id=device({"mp": mp + 1}), device_id_type=MESH)

    neighbours = 5 - (mp == 0).astype(jnp.int32) - (mp == 3).astype(jnp.int32)
    pl.semaphore_wait(barrier, neighbours)

    def part_of(owner, size):
        return pl.ds(pl.multiple_of(owner * size, size), size)

    half_rows = part_of(core, 2 * quarter)
    near_rows = part_of(seg, quarter)
    far_rows = part_of((seg + 2) % 4, quarter)
    rows_of_step = (half_rows, near_rows)

    def w_copy(step):
        local_block = seq if step == 0 else 1 - seq
        block = 2 * seq + local_block
        return pltpu.make_async_remote_copy(
            src_ref=w_out.at[rows_of_step[step], pl.ds(pl.multiple_of(local_block * width, width), width)],
            dst_ref=out_w.at[block, rows_of_step[step]],
            send_sem=w_ssem.at[step],
            recv_sem=w_rsem.at[step],
            device_id=device(seq_id),
            device_id_type=MESH,
        )

    def w_piece(i):
        block = 2 * seq + seq
        part = part_of(2 * core + i, quarter)
        return pltpu.make_async_remote_copy(
            src_ref=w_out.at[part, pl.ds(pl.multiple_of(seq * width, width), width)],
            dst_ref=out_w.at[block, part],
            send_sem=w_ssem.at[2 * i],
            recv_sem=w_rsem.at[2 * i],
            device_id=device(seq_id),
            device_id_type=MESH,
        )

    def w_first_wait():
        w_piece(0).wait_recv()
        w_piece(1).wait_recv()

    is_end = (mp == 0) | (mp == 3)
    first = jnp.where(mp < 2, 3, 0)
    third = 1 + seq
    late = 2 - seq
    inward = jnp.where(mp < 2, 1, 2)
    owns_first = (first // 2) == seq

    def end_w_direct(step):
        local_block = seq if step == 0 else 1 - seq
        return pltpu.make_async_remote_copy(
            src_ref=w_out.at[rows_of_step[step], pl.ds(pl.multiple_of(local_block * width, width), width)],
            dst_ref=end_w.at[step, rows_of_step[step]],
            send_sem=ew_ssem.at[step], recv_sem=ew_rsem.at[step],
            device_id=device({"mp": inward}), device_id_type=MESH,
        )

    def end_w_received(i):
        part = part_of(2 * core + i, quarter)
        return pltpu.make_async_remote_copy(
            src_ref=out_w.at[first, part],
            dst_ref=end_w.at[0, part],
            send_sem=ew_ssem.at[2 * i], recv_sem=ew_rsem.at[2 * i],
            device_id=device({"mp": inward}), device_id_type=MESH,
        )

    other = 1 - seq
    blocks = (
        out_w.at[2 * other + other],
        out_w.at[2 * other + 1 - other],
        end_w.at[0],
        end_w.at[1],
    )

    def cross_spread(b):
        return pltpu.make_async_remote_copy(
            src_ref=blocks[b].at[near_rows], dst_ref=blocks[b].at[near_rows],
            send_sem=wx_ssem.at[b], recv_sem=wx_rsem.at[b],
            device_id=device(cross_id), device_id_type=MESH,
        )

    def pair_spread(b, i):
        part = far_rows if i else (near_rows if b % 2 else half_rows)
        return pltpu.make_async_remote_copy(
            src_ref=blocks[b].at[part], dst_ref=blocks[b].at[part],
            send_sem=wp_ssem.at[b, i], recv_sem=wp_rsem.at[b, i],
            device_id=device(pair_id), device_id_type=MESH,
        )

    def spread_start(b):
        if b % 2:
            cross_spread(b).start()
        pair_spread(b, 0).start()

    def spread_far(b):
        cross_spread(b).wait_recv()
        pair_spread(b, 1).start()

    def spread_end(b):
        pair_spread(b, 0).wait_recv()
        if b % 2:
            pair_spread(b, 1).wait_recv()

    def spread_sent(b):
        pair_spread(b, 0).wait_send()
        if b % 2:
            cross_spread(b).wait_send()
            pair_spread(b, 1).wait_send()

    inner = jnp.logical_not(is_end)
    spreads_first = jnp.logical_not(is_end & jnp.logical_not(owns_first))

    def end_copy(j):
        return pltpu.make_async_remote_copy(
            src_ref=attended.at[j], dst_ref=end_rows.at[j],
            send_sem=end_ssem.at[j], recv_sem=end_rsem.at[j],
            device_id=device({"mp": inward}), device_id_type=MESH,
        )

    w_piece(0).start()

    @pl.when(is_end)
    def _():
        @pl.when(owns_first)
        def _():
            end_w_direct(0).start()

        end_w_direct(1).start()

    loads[0].wait()

    @pl.loop(0, caption_count)
    def _(c):
        values = cap_raw[c].astype(F32)
        scaled[c] = (values * gain[...]).astype(BF16)
        square = values * values
        folded = square[:, :HEAD]
        for group in range(1, features // HEAD):
            folded = folded + square[:, group * HEAD : (group + 1) * HEAD]
        squares[c] = folded.astype(BF16)

    loads[1].wait()
    loads[2].wait()
    tile = 256

    def slot_partial(u, out_core, dst):
        ids = [image_caption[4 * (2 * x + out_core) + u // 2] % caption_count for x in range(2)]
        lhs = jnp.concatenate([scaled[i] for i in ids], axis=0)
        half_index = u % 2

        @pl.loop(0, width // tile)
        def _(t):
            cols = pl.ds(pl.multiple_of(t * tile, tile), tile)
            part = jnp.dot(lhs, kv_w[half_index, :, cols], preferred_element_type=F32).astype(BF16)
            for x in range(2):
                dst[u, x, :, cols] = part[x * slots : (x + 1) * slots]

        for x in range(2):
            dst[u, x, :, width:] = squares[ids[x]]

    def pair_copy(j):
        return pltpu.make_async_remote_copy(
            src_ref=pair_send.at[j], dst_ref=pair_recv.at[j],
            send_sem=pair_ssem.at[j], recv_sem=pair_rsem.at[j],
            device_id=device(pair_id), device_id_type=MESH,
        )

    def cross_copy(j):
        return pltpu.make_async_remote_copy(
            src_ref=own.at[j, 1 - chip], dst_ref=cross_recv.at[j],
            send_sem=cross_ssem.at[j], recv_sem=cross_rsem.at[j],
            device_id=device(cross_id), device_id_type=MESH,
        )

    def row_copy(j):
        return pltpu.make_async_remote_copy(
            src_ref=rows.at[j, seq], dst_ref=rows.at[j, seq],
            send_sem=row_ssem.at[j], recv_sem=row_rsem.at[j],
            device_id=device(seq_id), device_id_type=MESH,
        )

    def stage_partial(j):
        slot_partial(j, 1 - core, pair_send)
        pair_copy(j).start()
        slot_partial(j, core, own)

    def stage_pair(j):
        pair_copy(j).wait_recv()
        far = 1 - chip
        own[j, far] = (own[j, far].astype(F32) + pair_recv[j, far].astype(F32)).astype(BF16)
        cross_copy(j).start()

    def stage_rows(j):
        cross_copy(j).wait_recv()
        tail = pl.ds(width, HEAD)
        mean = jnp.sum(
            own[j, chip, :, tail].astype(F32)
            + pair_recv[j, chip, :, tail].astype(F32)
            + cross_recv[j, :, tail].astype(F32),
            axis=1, keepdims=True,
        ) / total_features
        inverse = lax.rsqrt(mean + 1e-06)

        @pl.loop(0, width // tile)
        def _(t):
            cols = pl.ds(pl.multiple_of(t * tile, tile), tile)
            value = (
                own[j, chip, :, cols].astype(F32)
                + pair_recv[j, chip, :, cols].astype(F32)
                + cross_recv[j, :, cols].astype(F32)
            )
            rows[j, seq, :, cols] = (value * inverse).astype(BF16)

        row_copy(j).start()

    def stage_attend(j):
        row_copy(2 * j).wait_recv()
        row_copy(2 * j + 1).wait_recv()
        caption = image_caption[4 * seg + j]
        from_first = caption < caption_count
        live = caption_lengths[caption]
        mask = lax.broadcasted_iota(jnp.int32, (patches, slots), 1) < live

        def picked(u, cols):
            return jnp.where(from_first, rows[u, 0, :, cols], rows[u, 1, :, cols])

        for h in range(head_count):
            cols = slice(h * HEAD, (h + 1) * HEAD)
            scores = lax.dot_general(
                query_v[j, :, cols], picked(2 * j, cols),
                (((1,), (1,)), ((), ())), preferred_element_type=F32,
            ) * HEAD ** (-0.5)
            scores = jnp.where(mask, scores, -1e30)
            top = jnp.max(scores, axis=1, keepdims=True)
            expd = jnp.exp(scores - top)
            weights = (expd / jnp.sum(expd, axis=1, keepdims=True)).astype(BF16)
            attended[j, :, cols] = jnp.dot(
                weights, picked(2 * j + 1, cols), preferred_element_type=F32
            ).astype(BF16)

    def up_copy(n, j):
        return pltpu.make_async_remote_copy(
            src_ref=moving.at[n, j], dst_ref=moving.at[n, j],
            send_sem=z_ssem.at[n, j], recv_sem=z_rsem.at[n, j],
            device_id=device({"mp": lax.min(mp + 1, 3)}), device_id_type=MESH,
        )

    def down_copy(n, j):
        return pltpu.make_async_remote_copy(
            src_ref=moving.at[n, j], dst_ref=moving.at[n, j],
            send_sem=z_ssem.at[n, j], recv_sem=z_rsem.at[n, j],
            device_id=device({"mp": lax.max(mp - 1, 0)}), device_id_type=MESH,
        )

    def last_copy(n, j):
        return pltpu.make_async_remote_copy(
            src_ref=moving.at[n, j], dst_ref=from_right.at[j],
            send_sem=z_ssem.at[n, j], recv_sem=left_rsem.at[j],
            device_id=device({"mp": lax.max(mp - 1, 0)}), device_id_type=MESH,
        )

    def send_on(n, j):
        @pl.when(n > mp)
        def _():
            up_copy(n, j).start()

        @pl.when(n < mp - 1)
        def _():
            down_copy(n, j).start()

        @pl.when(n == mp - 1)
        def _():
            last_copy(n, j).start()

    def source_step(n, j):
        @pl.loop(0, width // tile)
        def _(t):
            cols = pl.ds(pl.multiple_of(t * tile, tile), tile)
            moving[n, j, :, cols] = jnp.dot(
                attended[j], out_w[n, :, cols], preferred_element_type=F32
            ).astype(BF16)

        send_on(n, j)

    def relay_step(n, j):
        up_copy(n, j).wait_recv()

        @pl.loop(0, width // tile)
        def _(t):
            cols = pl.ds(pl.multiple_of(t * tile, tile), tile)
            share = jnp.dot(attended[j], out_w[n, :, cols], preferred_element_type=F32)
            moving[n, j, :, cols] = (share + moving[n, j, :, cols].astype(F32)).astype(BF16)

        send_on(n, j)

    def joint_step(n, step, j):
        @pl.loop(0, width // tile)
        def _(t):
            cols = pl.ds(pl.multiple_of(t * tile, tile), tile)
            share = jnp.dot(attended[j], out_w[n, :, cols], preferred_element_type=F32)
            share = share + jnp.dot(end_rows[j], end_w[step, :, cols], preferred_element_type=F32)
            moving[n, j, :, cols] = share.astype(BF16)

        send_on(n, j)

    from_below = (mp > 0) & jnp.logical_not((mp == 1) & (third == 1))
    from_above = (mp < 3) & jnp.logical_not((mp == 2) & (third == 2))
    has_end_term = jnp.logical_not(is_end) & (third == mp)

    def final_step(j):
        @pl.when(from_below)
        def _():
            up_copy(mp, j).wait_recv()

        @pl.when(from_above)
        def _():
            last_copy(mp, j).wait_recv()

        def finish(t, terms):
            cols = pl.ds(pl.multiple_of(t * tile, tile), tile)
            share = jnp.dot(attended[j], out_w[mp, :, cols], preferred_element_type=F32)
            for term in terms:
                share = share + term(cols)
            result[j, :, cols] = (
                query_v[j, :, cols].astype(F32) + gate[pl.ds(j, 1), cols] * share
            ).astype(BF16)

        def below(cols):
            return moving[mp, j, :, cols].astype(F32)

        def above(cols):
            return from_right[j, :, cols].astype(F32)

        def end_term(cols):
            return jnp.dot(end_rows[j], end_w[1, :, cols], preferred_element_type=F32)

        for condition, terms in (
            (mp == 0, (above,)),
            (mp == 3, (below,)),
            (has_end_term & (mp == 1), (above, end_term)),
            (has_end_term & (mp == 2), (below, end_term)),
            (jnp.logical_not(is_end) & (third != mp), (below, above)),
        ):
            @pl.when(condition)
            def _():
                pl.loop(0, width // tile)(lambda t: finish(t, terms))

    def wait_send(n, j):
        up_copy(n, j).wait_send()

    near = inner & owns_first
    distant = inner & jnp.logical_not(owns_first)

    @pl.loop(0, rounds + 4)
    def _(u):
        @pl.when(u < rounds)
        def _():
            stage_partial(u)

        @pl.when((u >= 1) & (u < rounds + 1))
        def _():
            stage_pair(u - 1)

        @pl.when((u >= 2) & (u < rounds + 2))
        def _():
            stage_rows(u - 2)

        @pl.when(u == 1)
        def _():
            w_piece(1).start()

        for i in range(2):
            @pl.when((u == 2 + i) & is_end & jnp.logical_not(owns_first))
            def _():
                w_piece(i).wait_recv()
                end_w_received(i).start()

        @pl.when((u >= 4) & (u % 2 == 0))
        def _():
            j = (u - 4) // 2

            @pl.when(j == 0)
            def _():
                loads[3].wait()

            stage_attend(j)

            @pl.when(is_end)
            def _():
                end_copy(j).start()

        @pl.when((u == 4) & near)
        def _():
            end_w_direct(0).wait_recv()
            spread_start(2)
            end_w_direct(1).wait_recv()
            spread_start(3)

        @pl.when((u == 4) & spreads_first)
        def _():
            w_first_wait()
            spread_start(0)

        @pl.when((u == 4) & distant)
        def _():
            end_w_direct(1).wait_recv()
            spread_start(3)

        @pl.when(u == 8)
        def _():
            w_copy(1).wait_recv()
            spread_start(1)

        @pl.when(u == 10)
        def _():
            spread_far(1)

        @pl.when(u == 5)
        def _():
            w_copy(1).start()
            loads[4].wait()
            loads[5].wait()

            @pl.when(distant)
            def _():
                end_w_received(0).wait_recv()
                end_w_received(1).wait_recv()
                spread_start(2)

            @pl.when(spreads_first)
            def _():
                spread_end(0)

            @pl.when(inner)
            def _():
                spread_end(2)

        @pl.when((u >= 5) & (u % 2 == 1) & inner)
        def _():
            j = (u - 5) // 2
            end_copy(j).wait_recv()
            joint_step(first, 0, j)

            @pl.when(j == 0)
            def _():
                spread_far(3)
                spread_end(3)

            @pl.when(near)
            def _():
                joint_step(third, 1, j)

            @pl.when((j >= 1) & (j < images - 1))
            def _():
                relay_step(3 - first, j - 1)

    hidden_load.start()

    spread_end(1)

    @pl.when(is_end)
    def _():
        @pl.loop(0, images)
        def _(j):
            @pl.when(j >= 2)
            def _():
                wait_send(late, j - 2)

            source_step(late, j)

    @pl.when(inner)
    def _():
        @pl.loop(0, images + 2)
        def _(t):
            half_count = images // 2
            outward = (t == half_count) | (t == images + 1)
            late_j = t - (t > half_count).astype(jnp.int32)

            @pl.when(outward)
            def _():
                relay_step(3 - first, images - 2 + (t > half_count).astype(jnp.int32))

            @pl.when(jnp.logical_not(outward) & (late != mp))
            def _():
                relay_step(late, late_j)

    hidden_load.wait()

    @pl.loop(0, images)
    def _(j):
        final_step(j)

    for i in range(2):
        w_piece(i).wait_send()

    w_copy(1).wait_send()

    spread_sent(1)

    @pl.when(spreads_first)
    def _():
        spread_sent(0)

    @pl.loop(0, rounds)
    def _(u):
        pair_copy(u).wait_send()
        cross_copy(u).wait_send()
        row_copy(u).wait_send()

    @pl.when(is_end)
    def _():
        end_w_direct(1).wait_send()

        @pl.when(owns_first)
        def _():
            end_w_direct(0).wait_send()

        @pl.when(jnp.logical_not(owns_first))
        def _():
            end_w_received(0).wait_send()
            end_w_received(1).wait_send()

        for j in range(images):
            end_copy(j).wait_send()

        wait_send(late, images - 2)
        wait_send(late, images - 1)

    @pl.when(jnp.logical_not(is_end))
    def _():
        for step in range(2):
            spread_sent(2 + step)

        @pl.loop(0, images)
        def _(j):
            wait_send(first, j)
            wait_send(3 - first, j)

            @pl.when(third != mp)
            def _():
                wait_send(third, j)

            @pl.when(late != mp)
            def _():
                wait_send(late, j)


def fused_shards(
    captions,
    caption_lengths,
    image_caption,
    t5_gain,
    w_key,
    w_value,
    queries,
    hidden,
    out_gate,
    w_out,
):
    caption_count, slots, features = captions.shape
    images, patches, width = queries.shape
    packed = width + HEAD
    rounds = 2 * images
    smem = pl.BlockSpec(memory_space=pltpu.SMEM)
    vmem = pl.BlockSpec(memory_space=pltpu.VMEM)
    hbm = pl.BlockSpec(memory_space=pl.ANY)
    dma = pltpu.SemaphoreType.DMA
    return pl.pallas_call(
        fused_kernel,
        out_shape=jax.ShapeDtypeStruct(queries.shape, BF16),
        in_specs=[smem, smem, vmem, vmem, hbm, hbm, hbm, hbm, hbm, hbm],
        out_specs=vmem,
        scratch_shapes=[
            pltpu.VMEM(captions.shape, BF16),
            pltpu.VMEM((2,) + w_key.shape, BF16),
            pltpu.VMEM(queries.shape, BF16),
            pltpu.VMEM((4, w_out.shape[0], width), BF16),
            pltpu.VMEM(captions.shape, BF16),
            pltpu.VMEM((caption_count, slots, HEAD), BF16),
            pltpu.VMEM((rounds, 2, slots, packed), BF16),
            pltpu.VMEM((rounds, 2, slots, packed), BF16),
            pltpu.VMEM((rounds, 2, slots, packed), BF16),
            pltpu.VMEM((rounds, slots, packed), BF16),
            pltpu.VMEM((rounds, 2, slots, width), BF16),
            pltpu.VMEM(queries.shape, BF16),
            pltpu.VMEM((4,) + queries.shape, BF16),
            pltpu.VMEM(queries.shape, BF16),
            pltpu.VMEM(queries.shape, BF16),
            pltpu.VMEM((2, w_out.shape[0], width), BF16),
            dma((7,)),
            dma((rounds,)), dma((rounds,)),
            dma((rounds,)), dma((rounds,)),
            dma((rounds,)), dma((rounds,)),
            dma((3,)), dma((3,)),
            dma((4, images)), dma((4, images)), dma((images,)),
            dma((images,)), dma((images,)),
            dma((3,)), dma((3,)),
            dma((4,)), dma((4,)), dma((4, 2)), dma((4, 2)),
        ],
        compiler_params=pltpu.CompilerParams(
            collective_id=0, has_side_effects=True, vmem_limit_bytes=60 * 1024 * 1024
        ),
        cost_estimate=pl.CostEstimate(
            flops=20_000_000_000, bytes_accessed=20_000_000, transcendentals=1_100_000
        ),
    )(
        image_caption, caption_lengths, t5_gain.reshape(1, -1), out_gate,
        captions, w_key, w_value, queries, hidden, w_out,
    )


def solution(mesh):
    in_specs = (
        P("seq", None, "segment"),
        P(),
        P(),
        P("segment"),
        P("segment", "mp"),
        P("segment", "mp"),
        P("segment", "seq", "mp"),
        P("segment", "seq", "mp"),
        P("segment", "mp"),
        P("mp", "seq"),
    )
    out_specs = P("segment", "seq", "mp")
    fused = (mesh.shape["segment"], mesh.shape["seq"], mesh.shape["mp"]) == (4, 2, 4)
    shards = fused_shards if fused else general_shards
    return jax.shard_map(shards, mesh=mesh, in_specs=in_specs, out_specs=out_specs, check_vma=False)
```
